256 devices in a mesh: row: 32 (over z, y), col: 8 (over x, core).
Axes of the slice: x: 4, y: 4, z: 8, core: 2. Of those that a mesh axis runs over, the one named last changes fastest.
Arguments:
- tokens: bfloat16 [8192, 5376], P('row', 'col'), may hold values from -600 to 600, as said below
- input_gain: float32 [5376], P('col'), may hold values from 0.1 to 1.9
- q_gain: float32 [128], replicated, may hold values from 0.1 to 1.9
- k_gain: float32 [128], replicated, may hold values from 0.1 to 1.9
- wq: bfloat16 [5376, 2048], P('row', 'col'), may hold values from -0.078125 to 0.078125
- wk: bfloat16 [5376, 1024], P('row', 'col'), may hold values from -0.078125 to 0.078125
- wv: bfloat16 [5376, 1024], P('row', 'col'), may hold values from -0.078125 to 0.078125
- wo: bfloat16 [5376, 2048], P('row', 'col'), may hold values from -0.125 to 0.125
- upstream: bfloat16 [8192, 5376], P('row', 'col'), may hold values from -6 to 6
- doc_ids: int32 [8192], replicated, may hold values from 0 to 7, never falling along the last dimension, each value on 1 to 2048 neighbouring positions
- doc_labels: int32 [8], replicated, may hold values 0 or 1
Outputs:
- grad_input: bfloat16 [8192, 5376], P('row', 'col')
- grad_wq: bfloat16 [5376, 2048], P('row', 'col')
- grad_wk: bfloat16 [5376, 1024], P('row', 'col')
- grad_wv: bfloat16 [5376, 1024], P('row', 'col')
- grad_wo: bfloat16 [5376, 2048], P('row', 'col')
The draws below stay inside these ranges and needn't reach their ends.
Inputs may be any that keep to these rules, and one draw needn't show every extreme that they name: Activations whose scales differ between tokens and between features. `doc_ids`: documents are numbered in order along the pack; each has 1 to 2048 tokens and one has exactly 2048.
All inputs are finite; a program needn't handle non-finite values.
Results may differ from the reference program's by a relative error of at most 0.02.
Values may be sent and summed in bfloat16 or wider, within the bound.
A program may use at most 64 MiB of HBM per device.

```python
import math
import jax
import jax.numpy as jnp
import numpy as np
from jax import lax

D = 5376
HQ = 16
HK = 8
HD = 128
WIN = 1024
TOK_ROW = 256
TOKENS = 8192
HALO_DEV = 4
NDOC = 8
DOC_MOST = 2048
N_ROW = 32
N_COL = 8


def draw_tokens(key, part):
    key_rows, key_cols, key_base = jax.random.split(jax.random.fold_in(key, 11), 3)
    ramp = jnp.exp(jnp.linspace(jnp.log(0.3), jnp.log(3.0), D))
    col_scale = ramp * jnp.exp(jax.random.uniform(key_cols, (D,), minval=-0.3, maxval=0.3))
    base = jnp.clip(jax.random.normal(key_base, (TOKENS, D), jnp.float32), -6.0, 6.0)
    row_scale = jnp.exp(jax.random.uniform(key_rows, (TOKENS, 1), minval=0.0, maxval=jnp.log(10.0)))
    return (base * row_scale * col_scale[None, :]).astype(jnp.bfloat16)


def with_ends(entries, stream_key, smallest, high):
    extent = entries.shape
    place = [jax.random.randint(jax.random.fold_in(stream_key, axis), (), 0, extent[axis]) for axis in range(len(extent))]
    entries = entries.at[tuple(place)].set(smallest)
    longest = extent.index(max(extent))
    place[longest] = (place[longest] + 1) % extent[longest]
    return entries.at[tuple(place)].set(high)


def with_spikes(array, stream_key, source, target, blocks, factor):
    def block_of(position):
        return (jnp.arange(array.shape[position]) // (array.shape[position] // blocks)).reshape((-1,) + (1,) * (array.ndim - 1 - position))

    first = jax.random.permutation(stream_key, blocks)[block_of(target)]
    other_side = (block_of(target) + blocks // 2) % blocks
    return jnp.where((block_of(source) == first) | (block_of(source) == other_side), factor * array, array)


def shard_levels(key, dims, cuts, smallest, largest):
    def one(axis_at, shards_of):
        steps = jax.random.uniform(jax.random.fold_in(jax.random.fold_in(key, 6), axis_at), (shards_of,), jnp.float32, smallest / len(cuts), largest / len(cuts))
        return jnp.repeat(jnp.exp(steps), dims[axis_at] // shards_of).reshape((-1,) + (1,) * (len(dims) - axis_at - 1))

    factor_of = one(*cuts[0])
    for cut in cuts[1:]:
        factor_of = factor_of * one(*cut)
    return factor_of


def length_profile(count, total, limit, lean):
    weights = [(1 << 20) // math.isqrt(grade ** lean) + 1 for grade in range(2, count + 1)]
    spare, counts = total - limit - (count - 1), [1] * (count - 1)
    while spare > 0:
        movable = [i for i in range(count - 1) if counts[i] < limit]
        mass, remaining = sum([weights[i] for i in movable]), spare
        for i in movable:
            addition = min(limit - counts[i], max(1, remaining * weights[i] // mass), spare)
            counts[i] = counts[i] + addition
            spare = spare - addition
    return np.array([limit] + counts)


def ragged(own_key, number_of, total, reach, slope):
    if number_of == 2:
        one = jax.random.randint(own_key, (), max(1, total - reach), min(reach, total - 1) + 1)
        return jnp.stack([one, total - one])
    tallies = jnp.asarray(length_profile(number_of, total, reach, slope), jnp.int32)
    couples = (number_of - 1) // 2
    donor, sink = tallies[1:1 + 2 * couples:2], tallies[2:2 + 2 * couples:2]
    margin = jnp.minimum(donor - 1, reach - sink)
    shifted = jax.random.randint(jax.random.fold_in(own_key, 1), (couples,), 0, 1 << 20) % (margin + 1)
    tallies = tallies.at[1:1 + 2 * couples:2].set(donor - shifted).at[2:2 + 2 * couples:2].set(sink + shifted)
    return tallies[jax.random.permutation(jax.random.fold_in(own_key, 2), number_of)]


def bell_draw(key, shape, deviation, limit, shards=(), kind=jnp.bfloat16):
    entries = deviation * jax.random.normal(key, shape, jnp.float32)
    if shards:
        entries = entries * shard_levels(key, shape, shards, -0.22, 0.18)
    return jnp.clip(entries, -limit, limit).astype(kind)


def heavy_noise(rng, extent, spread, most, pieces, heavy, kind=jnp.bfloat16):
    entries = spread * jax.random.normal(rng, extent, jnp.float32)
    if pieces:
        entries = entries * shard_levels(rng, extent, pieces, -0.22, 0.18)
    return jnp.clip(with_spikes(entries, jax.random.fold_in(rng, 3), *heavy), -most, most).astype(kind)


def setup_inputs(seed: int = 0) -> dict:
    streams_of = jax.random.split(jax.random.key(seed), 12)
    return {
        "tokens": draw_tokens(jax.random.fold_in(streams_of[11], 71), 0),
        "input_gain": jnp.clip(1.0 + 0.18 * jax.random.normal(streams_of[1], (D,), jnp.float32), 0.1, 1.9),
        "q_gain": jnp.clip(1.0 + 0.18 * jax.random.normal(streams_of[2], (HD,), jnp.float32), 0.1, 1.9),
        "k_gain": jnp.clip(1.0 + 0.18 * jax.random.normal(streams_of[3], (HD,), jnp.float32), 0.1, 1.9),
        "wq": bell_draw(streams_of[4], (D, HQ * HD), D ** -0.5, 0.078125, ((0, 32), (1, 8))),
        "wk": bell_draw(streams_of[5], (D, HK * HD), D ** -0.5, 0.078125, ((0, 32), (1, 8))),
        "wv": bell_draw(streams_of[6], (D, HK * HD), D ** -0.5, 0.078125, ((0, 32), (1, 8))),
        "wo": bell_draw(streams_of[7], (D, HQ * HD), (HQ * HD) ** -0.5, 0.125, ((0, 32), (1, 8))),
        "upstream": heavy_noise(streams_of[8], (TOKENS, D), 1.0, 6.0, ((0, 32), (1, 8)), (0, 1, 32, 2.75)),
        "doc_ids": jnp.searchsorted(jnp.cumsum(ragged(streams_of[9], NDOC, TOKENS, DOC_MOST, 1)), jnp.arange(TOKENS), side="right").astype(jnp.int32),
        "doc_labels": with_ends((jax.random.randint(streams_of[10], (NDOC,), 0, 2) < 1).astype(jnp.int32), jax.random.fold_in(streams_of[10], 1), 0, 1),
    }


epsilon = 1e-06
query_scale = 168.0 ** (-0.5)

def rope_tables(positions):
    half_size = HD // 2
    frequency = 10000.0 ** (-(2.0 * jnp.arange(half_size, dtype=jnp.float32)) / HD)
    angles = positions[:, None] * frequency[None, :]
    return (jnp.cos(angles)[:, None, :], jnp.sin(angles)[:, None, :])

def rotate(values_in, cosine, sine):
    half_size = values_in.shape[-1] // 2
    first_half = values_in[..., :half_size]
    second_half = values_in[..., half_size:]
    return jnp.concatenate([first_half * cosine - second_half * sine, second_half * cosine + first_half * sine], -1)

def rotate_back(grads_in, cosine, sine):
    half_size = grads_in.shape[-1] // 2
    first_half = grads_in[..., :half_size]
    second_half = grads_in[..., half_size:]
    return jnp.concatenate([first_half * cosine + second_half * sine, second_half * cosine - first_half * sine], -1)

def head_norm(values_in):
    scaling = lax.rsqrt(lax.optimization_barrier(jnp.mean(values_in * values_in, -1, keepdims=True)) + epsilon)
    return (values_in * scaling, scaling)

def head_norm_back(grad_unit, unit_values, scaling):
    return scaling * (grad_unit - unit_values * lax.optimization_barrier(jnp.mean(grad_unit * unit_values, -1, keepdims=True)))

def attend(queries, keys_in, values_in, d_attn, allowed):
    f32 = jnp.float32
    scores = jnp.einsum('tkgd,skd->kgts', queries.astype(f32), keys_in.astype(f32))
    weights = jnp.where(allowed[None, None], jnp.exp(scores), 0.0)
    probs = weights / lax.optimization_barrier(jnp.sum(weights, -1, keepdims=True))
    probs_low = probs.astype(jnp.bfloat16)
    attended = jnp.einsum('kgts,skd->tkgd', probs_low.astype(f32), values_in.astype(f32)).astype(jnp.bfloat16)
    d_prob = jnp.einsum('tkgd,skd->kgts', d_attn.astype(f32), values_in.astype(f32))
    delta = lax.optimization_barrier(jnp.sum(probs * d_prob, -1, keepdims=True))
    d_score = (probs * (d_prob - delta)).astype(jnp.bfloat16)
    d_query = jnp.einsum('kgts,skd->tkgd', d_score.astype(f32), keys_in.astype(f32))
    d_key = jnp.einsum('kgts,tkgd->skd', d_score.astype(f32), queries.astype(f32))
    d_value = jnp.einsum('kgts,tkgd->skd', probs_low.astype(f32), d_attn.astype(f32))
    return (attended, d_query, d_key, d_value)

def block_sum(left_rows, right_rows):
    left_blocks = left_rows.reshape(N_ROW, TOK_ROW, left_rows.shape[1])
    right_blocks = right_rows.reshape(N_ROW, TOK_ROW, right_rows.shape[1])

    def add_block(carried, pair):
        piece_sum = jnp.dot(pair[0].T, pair[1], preferred_element_type=jnp.float32).astype(jnp.bfloat16)
        piece_sum = lax.optimization_barrier(piece_sum)
        return (carried + piece_sum.astype(jnp.float32), None)
    start_sum = jnp.zeros((left_rows.shape[1], right_rows.shape[1]), jnp.float32)
    summed, unused = lax.scan(add_block, start_sum, (left_blocks, right_blocks))
    return summed.astype(jnp.bfloat16)

def reference(tokens, input_gain, q_gain, k_gain, wq, wk, wv, wo, upstream, doc_ids, doc_labels):
    f32 = jnp.float32
    bf16 = jnp.bfloat16
    features = tokens.astype(f32)
    scale_in = lax.rsqrt(lax.optimization_barrier(jnp.mean(features * features, 1, keepdims=True)) + epsilon)
    unit_in = features * scale_in
    normed = (unit_in * input_gain).astype(bf16)
    group_size = HQ // HK
    q_proj = jnp.dot(normed, wq, preferred_element_type=f32).reshape(TOKENS, HQ, HD)
    k_proj = jnp.dot(normed, wk, preferred_element_type=f32).reshape(TOKENS, HK, HD)
    values = jnp.dot(normed, wv, preferred_element_type=f32).astype(bf16).reshape(TOKENS, HK, HD)
    positions = jnp.arange(TOKENS, dtype=jnp.int32).astype(f32)
    cosine, sine = rope_tables(positions)
    unit_q, scale_q = head_norm(q_proj)
    query = (rotate(unit_q * q_gain, cosine, sine) * query_scale).astype(bf16)
    unit_k, scale_k = head_norm(k_proj)
    key = rotate(unit_k * k_gain, cosine, sine).astype(bf16)
    member = (doc_ids[:, None] == jnp.arange(NDOC, dtype=jnp.int32)[None, :]).astype(jnp.int32)
    forget = lax.optimization_barrier(jnp.sum(member * doc_labels[None, :], 1))
    token_sign = (1 - 2 * forget).astype(f32)
    cotangent = (token_sign[:, None] * upstream.astype(f32)).astype(bf16)
    d_attn = jnp.dot(cotangent, wo, preferred_element_type=f32).astype(bf16)
    reach_rows = HALO_DEV * TOK_ROW
    key_span = reach_rows + TOK_ROW
    key_pad = jnp.concatenate([jnp.zeros((reach_rows, HK, HD), bf16), key], 0)
    value_pad = jnp.concatenate([jnp.zeros((reach_rows, HK, HD), bf16), values], 0)
    doc_pad = jnp.concatenate([jnp.full((reach_rows,), -1, jnp.int32), doc_ids], 0)

    def block_step(carried, block_index):
        grad_keys, grad_values = carried
        first_row = (block_index * TOK_ROW).astype(jnp.int32)
        query_block = lax.dynamic_slice_in_dim(query, first_row, TOK_ROW, 0).reshape(TOK_ROW, HK, group_size, HD)
        attn_grad_block = lax.dynamic_slice_in_dim(d_attn, first_row, TOK_ROW, 0).reshape(TOK_ROW, HK, group_size, HD)
        key_block = lax.dynamic_slice_in_dim(key_pad, first_row, key_span, 0)
        value_block = lax.dynamic_slice_in_dim(value_pad, first_row, key_span, 0)
        doc_keys = lax.dynamic_slice_in_dim(doc_pad, first_row, key_span, 0)
        doc_queries = lax.dynamic_slice_in_dim(doc_ids, first_row, TOK_ROW, 0)
        query_pos = first_row + jnp.arange(TOK_ROW, dtype=jnp.int32)
        key_pos = first_row - reach_rows + jnp.arange(key_span, dtype=jnp.int32)
        distance = query_pos[:, None] - key_pos[None, :]
        allowed = (distance >= 0) & (distance < WIN) & (key_pos[None, :] >= 0) & (doc_queries[:, None] == doc_keys[None, :])
        attended, d_query, d_key, d_value = attend(query_block, key_block, value_block, attn_grad_block, allowed)
        grad_keys = lax.dynamic_update_slice_in_dim(grad_keys, lax.dynamic_slice_in_dim(grad_keys, first_row, key_span, 0) + d_key, first_row, 0)
        grad_values = lax.dynamic_update_slice_in_dim(grad_values, lax.dynamic_slice_in_dim(grad_values, first_row, key_span, 0) + d_value, first_row, 0)
        return ((grad_keys, grad_values), (attended.reshape(TOK_ROW, HQ * HD), d_query.reshape(TOK_ROW, HQ, HD)))
    start_grads = (jnp.zeros((reach_rows + TOKENS, HK, HD), f32), jnp.zeros((reach_rows + TOKENS, HK, HD), f32))
    (grad_keys, grad_values), (attn, d_query) = lax.scan(block_step, start_grads, jnp.arange(N_ROW, dtype=jnp.int32))
    attn = attn.reshape(TOKENS, HQ * HD)
    d_query = d_query.reshape(TOKENS, HQ, HD)
    d_key = grad_keys[reach_rows:]
    grad_v_act = grad_values[reach_rows:].astype(bf16).reshape(TOKENS, HK * HD)
    grad_q_act = head_norm_back(rotate_back(d_query, cosine, sine) * query_scale * q_gain, unit_q, scale_q).astype(bf16).reshape(TOKENS, HQ * HD)
    grad_k_act = head_norm_back(rotate_back(d_key, cosine, sine) * k_gain, unit_k, scale_k).astype(bf16).reshape(TOKENS, HK * HD)
    q_group = HQ * HD // N_COL
    k_group = HK * HD // N_COL
    d_normed = jnp.zeros((TOKENS, D), f32)
    for column in range(N_COL):
        q_cols = slice(column * q_group, (column + 1) * q_group)
        k_cols = slice(column * k_group, (column + 1) * k_group)
        term = jnp.dot(grad_q_act[:, q_cols], wq[:, q_cols].T, preferred_element_type=f32)
        term = term + jnp.dot(grad_k_act[:, k_cols], wk[:, k_cols].T, preferred_element_type=f32)
        term = term + jnp.dot(grad_v_act[:, k_cols], wv[:, k_cols].T, preferred_element_type=f32)
        term = lax.optimization_barrier(term.astype(bf16))
        d_normed = d_normed + term.astype(f32)
    scaled_grad = d_normed * input_gain
    grad_input = (scale_in * (scaled_grad - unit_in * lax.optimization_barrier(jnp.mean(scaled_grad * unit_in, 1, keepdims=True)))).astype(bf16)
    grad_wq = block_sum(normed, grad_q_act)
    grad_wk = block_sum(normed, grad_k_act)
    grad_wv = block_sum(normed, grad_v_act)
    grad_wo = block_sum(cotangent, attn)
    return (grad_input, grad_wq, grad_wk, grad_wv, grad_wo)
```

```python
import jax
import jax.numpy as jnp
from jax import lax
from jax.sharding import Mesh
from jax.sharding import PartitionSpec as P

D = 5376
HD = 128
WIN = 1024
epsilon = 1e-06
query_scale = 168.0 ** (-0.5)
f32 = jnp.float32
bf16 = jnp.bfloat16


def tables(row, tok):
    half = HD // 2
    positions = (row * tok + jnp.arange(tok, dtype=jnp.int32)).astype(f32)
    frequency = 10000.0 ** (-(2.0 * jnp.arange(half, dtype=f32)) / HD)
    angles = frequency[:, None] * positions[None, :]
    return jnp.cos(angles), jnp.sin(angles)


def rot(v, c, s):
    a, b = v[: HD // 2], v[HD // 2 :]
    return jnp.concatenate([a * c - b * s, b * c + a * s], 0)


def unit(p):
    sc = lax.rsqrt(jnp.mean(p * p, 0, keepdims=True) + epsilon)
    return p * sc, sc


def unit_back(w, u, sc):
    return sc * (w - u * jnp.mean(w * u, 0, keepdims=True))


def per_device(tokens, input_gain, q_gain, k_gain, wq, wk, wv, wo, upstream, doc_ids, doc_labels):
    tok = tokens.shape[0]
    nz, ny = lax.axis_size("z"), lax.axis_size("y")
    nrow = nz * ny
    row = lax.axis_index("z") * ny + lax.axis_index("y")
    col = ("x", "k")
    fr = wq.shape[0]
    x32 = tokens.astype(f32)
    ss = lax.psum(jnp.sum(x32 * x32, 1), col)
    scale = lax.rsqrt(ss / D + epsilon)[None, :]
    docs = lax.dynamic_slice_in_dim(doc_ids, row * tok, tok, 0)
    member = (docs[:, None] == jnp.arange(doc_labels.shape[0], dtype=jnp.int32)[None, :]).astype(jnp.int32)
    sign = (1 - 2 * jnp.sum(member * doc_labels[None, :], 1)).astype(f32)
    before = jnp.sum((doc_ids[None, :] < jnp.arange(doc_labels.shape[0])[:, None]).astype(jnp.int32), 1)
    start = jnp.sum(member * before[None, :], 1)
    pos = row * tok + jnp.arange(tok, dtype=jnp.int32)
    low = jnp.maximum(start, pos - (WIN - 1))
    xg = (x32 * input_gain).astype(bf16).T.reshape(ny, fr, tok)
    ct = (upstream.astype(f32) * sign[:, None]).astype(bf16).T.reshape(ny, fr, tok)
    xa = lax.all_to_all(xg, "y", 0, 0)
    ca = lax.all_to_all(ct, "y", 0, 0)
    X = lax.all_gather(xa, col)
    C = lax.all_gather(ca, col)
    W = lax.all_gather(jnp.concatenate([wq, wk, wv, wo], 1), "z")
    qkv = jnp.einsum("cfh,cyft->yht", W[:, :, :512], X, preferred_element_type=f32).astype(bf16)
    dat = jnp.einsum("cfh,cyft->yht", W[:, :, 512:], C, preferred_element_type=f32).astype(bf16)
    proj = lax.psum_scatter(qkv, "y", scatter_dimension=0).astype(f32) * scale
    dA = lax.psum_scatter(dat, "y", scatter_dimension=0).astype(bf16)
    c, s = tables(row, tok)
    qgc, kgc = q_gain[:, None], k_gain[:, None]
    uq0, sq0 = unit(proj[:128])
    uq1, sq1 = unit(proj[128:256])
    uk, sk = unit(proj[256:384])
    vT = proj[384:].astype(bf16)
    q = jnp.concatenate([rot(uq0 * qgc, c, s), rot(uq1 * qgc, c, s)], 1) * query_scale
    q = q.astype(bf16)
    da = jnp.concatenate([dA[:128], dA[128:]], 1)
    kT = rot(uk * kgc, c, s).astype(bf16)
    kv = jnp.stack([kT, vT])
    blocks = [kv]
    for d in range(1, 5):
        route = [(i, (i + d) % nrow) for i in range(nrow)]
        blocks.append(lax.ppermute(kv, ("z", "y"), route))
    low2 = jnp.concatenate([low, low])[None, :]
    pos2 = jnp.concatenate([pos, pos])[None, :]
    es = []
    total = 0.0
    for d in range(5):
        sp = ((row - d) * tok + jnp.arange(tok, dtype=jnp.int32))[:, None]
        ok = (sp >= low2) & (sp <= pos2)
        sc = jnp.einsum("ds,dt->st", blocks[d][0], q, preferred_element_type=f32)
        e = jnp.where(ok, jnp.exp(sc), 0.0)
        es.append(e)
        total = total + jnp.sum(e, 0, keepdims=True)
    inv = 1.0 / total
    attn = 0.0
    for d in range(5):
        attn = attn + jnp.einsum("ds,st->dt", blocks[d][1], (es[d] * inv).astype(bf16), preferred_element_type=f32)
    delta = jnp.sum(attn * da.astype(f32), 0, keepdims=True)
    dq = 0.0
    dkv = 0.0
    for d in range(5):
        p = es[d] * inv
        dp = jnp.einsum("ds,dt->st", blocks[d][1], da, preferred_element_type=f32)
        ds = (p * (dp - delta)).astype(bf16)
        dq = dq + jnp.einsum("ds,st->dt", blocks[d][0], ds, preferred_element_type=f32)
        dk = jnp.einsum("dt,st->ds", q, ds, preferred_element_type=f32)
        dv = jnp.einsum("dt,st->ds", da, p.astype(bf16), preferred_element_type=f32)
        part = jnp.stack([dk, dv])
        if d:
            route = [(i, (i - d) % nrow) for i in range(nrow)]
            part = lax.ppermute(part.astype(bf16), ("z", "y"), route).astype(f32)
        dkv = dkv + part
    g0 = unit_back(rot(dq[:, :tok], c, -s) * query_scale * qgc, uq0, sq0)
    g1 = unit_back(rot(dq[:, tok:], c, -s) * query_scale * qgc, uq1, sq1)
    gk = unit_back(rot(dkv[0], c, -s) * kgc, uk, sk)
    G = jnp.concatenate([g0, g1, gk, dkv[1]], 0) * scale
    inner = lax.psum(jnp.sum(G * proj, 0), col) / D
    at = jnp.concatenate([attn[:, :tok], attn[:, tok:]], 0).astype(bf16)
    GA = lax.all_gather(jnp.concatenate([G.astype(bf16), at], 0), "y")
    dn = jnp.einsum("cfh,yht->cyft", W[:, :, :512], GA[:, :512], preferred_element_type=f32).astype(bf16)
    dn = lax.psum_scatter(dn.reshape(8, ny, fr, tok), col, scatter_dimension=0)
    dn = lax.all_to_all(dn, "y", 0, 0).reshape(ny * fr, tok).astype(f32).T
    grad_input = (dn * input_gain - x32 * scale[0][:, None] * inner[:, None]).astype(bf16)
    dw = jnp.einsum("cyft,yht->cfh", X, GA[:, :512], preferred_element_type=f32)
    dwo = jnp.einsum("cyft,yht->cfh", C, GA[:, 512:], preferred_element_type=f32)
    dw = lax.psum_scatter(jnp.concatenate([dw, dwo], 2).astype(bf16), "z", scatter_dimension=0)
    return grad_input, dw[:, :256], dw[:, 256:384], dw[:, 384:512], dw[:, 512:]


def solution(mesh):
    fine = Mesh(mesh.devices.reshape(8, 4, 4, 2), ("z", "y", "x", "k"))
    rc = P(("z", "y"), ("x", "k"))
    return jax.shard_map(
        per_device,
        mesh=fine,
        in_specs=(rc, P(("x", "k")), P(), P(), rc, rc, rc, rc, rc, P(), P()),
        out_specs=(rc,) * 5,
        check_vma=False,
    )
```

```python
import jax
import jax.numpy as jnp
from jax import lax
from jax.experimental import pallas as pl
from jax.experimental.pallas import tpu as pltpu
from jax.sharding import Mesh
from jax.sharding import PartitionSpec as P

D = 5376
HD = 128
WIN = 1024
NZ, NY, NX, NK = 8, 4, 4, 2
NC = NX * NK
TOK = 256
FR = 168
NDOC = 8
NSEM = 240
epsilon = 1e-06
query_scale = 168.0 ** (-0.5)
f32 = jnp.float32
bf16 = jnp.bfloat16
MESH = pl.DeviceIdType.MESH


def dot(a, b, ca, cb):
    return lax.dot_general(a, b, (((ca,), (cb,)), ((), ())), preferred_element_type=f32)


def eye(n):
    return (lax.broadcasted_iota(jnp.int32, (n, n), 0) == lax.broadcasted_iota(jnp.int32, (n, n), 1)).astype(bf16)


def rot(v, c, s):
    a, b = v[: HD // 2], v[HD // 2 :]
    return jnp.concatenate([a * c - b * s, b * c + a * s], 0)


def unit(p):
    sc = lax.rsqrt(jnp.mean(p * p, 0, keepdims=True) + epsilon)
    return p * sc, sc


def unit_back(w, u, sc):
    return sc * (w - u * jnp.mean(w * u, 0, keepdims=True))


def kernel(
    tokens, upstream, gain, q_gain, k_gain, wq, wk, wv, wo, cos_t, sin_t, docs, labels,
    g_in, g_wq, g_wk, g_wv, g_wo,
    xsrc, csrc, X, C, Wp, Wo, ssq, inn, raw,
    pq, pr, prh, oq, orr, orh,
    KV, ex, dsb, drb, A, Gq, Gk,
    hb, hr, sb, rb,
    nb, nr, mh, mrh, mb, mr, ds_, dr_, dn,
    sem_s, sem_r,
):
    z, y, x, k = (lax.axis_index(n) for n in ("z", "y", "x", "k"))
    c = x * NK + k
    row = z * NY + y
    zi = [lax.rem(z + r, NZ) for r in range(NZ)]
    yi = [lax.rem(y + r, NY) for r in range(NY)]
    xi = [lax.rem(x + r, NX) for r in range(NX)]
    ko = 1 - k
    rows = {}
    for d in (1, 2, 3, 4, -1, -2, -3, -4):
        rr = lax.rem(row + d + NZ * NY, NZ * NY)
        rows[d] = {"z": rr // NY, "y": lax.rem(rr, NY)}
    cols = []
    for d in range(1, NC):
        cc = lax.rem(c + d, NC)
        cols.append({"x": cc // NK, "k": lax.rem(cc, NK)})

    barrier = pltpu.get_barrier_semaphore()
    for dev in list(rows.values()) + cols:
        pl.semaphore_signal(barrier, inc=1, device_id=dev, device_id_type=MESH)

    count = [0]
    started = []

    def send(src, dst, dev):
        i = count[0]
        count[0] += 1
        copy = pltpu.make_async_remote_copy(
            src_ref=src, dst_ref=dst, send_sem=sem_s.at[i], recv_sem=sem_r.at[i],
            device_id=dev, device_id_type=MESH,
        )
        copy.start()
        started.append(copy)
        return copy

    zp, zm = {"z": zi[1]}, {"z": zi[NZ - 1]}
    yp, ym = {"y": yi[1]}, {"y": yi[NY - 1]}
    xp, xm = {"x": xi[1]}, {"x": xi[NX - 1]}
    sib = {"k": ko}

    Wp[z, :, 0:256] = wq[...]
    Wp[z, :, 256:384] = wk[...]
    Wp[z, :, 384:512] = wv[...]
    Wo[z] = wo[...]
    pl.semaphore_wait(barrier, len(rows) + len(cols))

    def ring_start(W):
        return [send(W.at[z], W.at[z], zp)], [send(W.at[z], W.at[z], zm)]

    def ring_step(W, fwd, bwd, half):
        s = len(fwd)
        zf, zb = zi[NZ - s], zi[s]
        fwd[-1].wait_recv()
        if s < 3:
            fwd.append(send(W.at[zf], W.at[zf], zp))
        elif s == 3:
            fwd.append(send(W.at[zf, :, pl.ds(0, half)], W.at[zf, :, pl.ds(0, half)], zp))
        bwd[-1].wait_recv()
        if s < 3:
            bwd.append(send(W.at[zb], W.at[zb], zm))
        elif s == 3:
            bwd.append(send(W.at[zb, :, pl.ds(half, half)], W.at[zb, :, pl.ds(half, half)], zm))

    ring_p = ring_start(Wp)

    raw[...] = dot(eye(NY * FR), tokens[...], 1, 1)
    x32 = raw[...]
    own_sq = jnp.sum(x32 * x32, 0, keepdims=True)
    ssq[c] = jnp.broadcast_to(own_sq, (8, TOK))
    for i in range(NY):
        xsrc[i] = (raw[i * FR : (i + 1) * FR] * gain[i * FR : (i + 1) * FR]).astype(bf16)

    def exchange(src, Y):
        out = {}
        for e in (2, 1, 3):
            out[e] = send(src.at[yi[e]], Y.at[c, y], {"y": yi[e]})
        Y[c, y] = src[yi[0]]
        return out

    a2x = exchange(xsrc, X)

    def spread(Y, e, far):
        ref = Y.at[c, yi[e]]
        far["p", e] = send(ref, ref, xp)
        far["m", e] = send(ref, ref, xm)
        far["s", 0, e] = send(ref, ref, sib)

    def onward(Y, e, far):
        left = Y.at[xi[NX - 1] * NK + k, yi[e]]
        right = Y.at[xi[1] * NK + k, yi[e]]
        far["p", e].wait_recv()
        if e in (0, 1):
            far["f", e] = send(left, left, xp)
        far["s", 1, e] = send(left, left, sib)
        far["m", e].wait_recv()
        if e in (2, 3):
            far["f", e] = send(right, right, xm)
        far["s", 2, e] = send(right, right, sib)

    def across(Y, e, far):
        ref = Y.at[xi[2] * NK + k, yi[e]]
        far["f", e].wait_recv()
        far["s", 3, e] = send(ref, ref, sib)

    def gathered(far):
        for i in range(4):
            for e in range(NY):
                far["s", i, e].wait_recv()

    fx, fc = {}, {}
    spread(X, 0, fx)
    sq_sent = [send(ssq.at[c], ssq.at[c], dev) for dev in cols]

    own_docs = docs[pl.ds(row, 1), :].astype(f32)
    all_docs = docs[...].astype(f32)
    sign = jnp.ones((1, TOK), f32)
    start = jnp.zeros((1, TOK), f32)
    for d in range(NDOC):
        member = (own_docs == d).astype(f32)
        sign = sign - 2.0 * member * labels[d].astype(f32)
        start = start + member * jnp.sum(
            jnp.sum((all_docs < d).astype(f32), 0, keepdims=True), 1, keepdims=True
        )
    lane = lax.broadcasted_iota(jnp.int32, (1, TOK), 1).astype(f32)
    low = jnp.maximum(start - (row * TOK).astype(f32), lane - (WIN - 1.0))
    up_t = dot(eye(NY * FR), upstream[...], 1, 1)
    for i in range(NY):
        csrc[i] = (up_t[i * FR : (i + 1) * FR] * sign).astype(bf16)

    for e in (1, 3):
        a2x[4 - e].wait_recv()
        spread(X, e, fx)
    ring_step(Wp, *ring_p, 256)
    a2x[2].wait_recv()
    spread(X, 2, fx)
    a2c = exchange(csrc, C)
    onward(X, 0, fx)
    onward(X, 1, fx)
    ring_step(Wp, *ring_p, 256)
    onward(X, 3, fx)
    onward(X, 2, fx)
    ring_step(Wp, *ring_p, 256)
    ring_o = ring_start(Wo)
    for e in (0, 1, 3):
        across(X, e, fx)
    spread(C, 0, fc)
    across(X, 2, fx)
    for e in (1, 3, 2):
        a2c[4 - e].wait_recv()
        spread(C, e, fc)
    gathered(fx)
    ring_step(Wp, *ring_p, 256)

    def partial(W, Y, e):
        total = None
        for i in range(NC):
            t = dot(W[i], Y[i, yi[e]], 0, 0)
            total = t if total is None else total + t
        return total

    def reduce_far(W, Y, buf, got, n):
        buf[0] = partial(W, Y, 2).astype(bf16)
        h = n // 2
        return (
            send(buf.at[0, pl.ds(0, h)], got.at[0], yp),
            send(buf.at[0, pl.ds(h, h)], got.at[1], ym),
        )

    def reduce_near(W, Y, buf, got, full, n, sent):
        h = n // 2
        t = partial(W, Y, 1)
        sent[0].wait_recv()
        buf[1, 0:h] = (t[0:h] + got[0].astype(f32)).astype(bf16)
        buf[1, h:n] = t[h:n].astype(bf16)
        a = send(buf.at[1], full.at[0], yp)
        t = partial(W, Y, 3)
        sent[1].wait_recv()
        buf[2, 0:h] = t[0:h].astype(bf16)
        buf[2, h:n] = (t[h:n] + got[1].astype(f32)).astype(bf16)
        b = send(buf.at[2], full.at[1], ym)
        return a, b

    far_q = reduce_far(Wp, X, pq, prh, 512)
    onward(C, 0, fc)
    near_q = reduce_near(Wp, X, pq, prh, pr, 512, far_q)
    ring_step(Wo, *ring_o, 128)
    onward(C, 1, fc)
    onward(C, 3, fc)
    own_q = partial(Wp, X, 0)
    ring_step(Wo, *ring_o, 128)
    onward(C, 2, fc)
    for s in sq_sent:
        s.wait_recv()
    total_sq = ssq[0, 0:1]
    for i in range(1, NC):
        total_sq = total_sq + ssq[i, 0:1]
    scale = lax.rsqrt(total_sq / D + epsilon)
    near_q[0].wait_recv()
    near_q[1].wait_recv()
    proj = (own_q + pr[0].astype(f32) + pr[1].astype(f32)) * scale
    co, si = cos_t[...], sin_t[...]
    qg, kg = q_gain[...], k_gain[...]
    uq0, sq0 = unit(proj[0:128])
    uq1, sq1 = unit(proj[128:256])
    uk, sk = unit(proj[256:384])
    q = jnp.concatenate([rot(uq0 * qg, co, si), rot(uq1 * qg, co, si)], 1) * query_scale
    q = q.astype(bf16)
    KV[0, 0:128] = rot(uk * kg, co, si).astype(bf16)
    KV[0, 128:256] = proj[384:512].astype(bf16)
    kv_sent = {d: send(KV.at[0], KV.at[d], rows[d]) for d in (4, 1, 2, 3)}
    ring_step(Wo, *ring_o, 128)
    for e in (0, 1, 3, 2):
        across(C, e, fc)
    ring_step(Wo, *ring_o, 128)
    gathered(fc)
    far_o = reduce_far(Wo, C, oq, orh, 256)
    near_o = reduce_near(Wo, C, oq, orh, orr, 256, far_o)
    own_o = partial(Wo, C, 0)

    low2 = jnp.concatenate([low, low], 1)
    at2 = jnp.concatenate([lane, lane], 1)
    below = lax.broadcasted_iota(jnp.int32, (TOK, 2 * TOK), 0).astype(f32)
    total = jnp.zeros((1, 2 * TOK), f32)
    attn = jnp.zeros((HD, 2 * TOK), f32)
    for d in (0, 1, 4, 3, 2):
        if d:
            kv_sent[d].wait_recv()
        s = dot(KV[d, 0:128], q, 0, 0)
        ok = below >= low2 + d * TOK
        if d == 0:
            ok = ok & (below <= at2)
        e = jnp.where(ok, jnp.exp(s), 0.0)
        ex[d] = e
        total = total + jnp.sum(e, 0, keepdims=True)
        attn = attn + dot(KV[d, 128:256], e.astype(bf16), 1, 0)
    inv = 1.0 / total
    attn = attn * inv
    A[y, 0:128] = attn[:, 0:TOK].astype(bf16)
    A[y, 128:256] = attn[:, TOK:].astype(bf16)

    def ag_start(B):
        return [send(B.at[y], B.at[y], yp), send(B.at[y], B.at[y], ym)]

    def ag_step(B, s):
        s[0].wait_recv()
        low_half = B.at[yi[3], pl.ds(0, 128)]
        s.append(send(low_half, low_half, yp))
        s[1].wait_recv()
        high_half = B.at[yi[1], pl.ds(128, 128)]
        s.append(send(high_half, high_half, ym))

    def ag_end(s):
        s[2].wait_recv()
        s[3].wait_recv()

    ag_a = ag_start(A)
    near_o[0].wait_recv()
    near_o[1].wait_recv()
    da = own_o + orr[0].astype(f32) + orr[1].astype(f32)
    da = jnp.concatenate([da[0:128], da[128:256]], 1).astype(bf16)
    delta = jnp.sum(attn * da.astype(f32), 0, keepdims=True)
    dq = jnp.zeros((HD, 2 * TOK), f32)
    dkv_sent = {}
    for d in (4, 2, 3, 1, 0):
        p = ex[d] * inv
        dp = dot(KV[d, 128:256], da, 0, 0)
        ds = (p * (dp - delta)).astype(bf16)
        dq = dq + dot(KV[d, 0:128], ds, 1, 0)
        dk = dot(q, ds, 1, 1)
        dv = dot(da, p.astype(bf16), 1, 1)
        if d:
            dsb[d - 1, 0:128] = dk.astype(bf16)
            dsb[d - 1, 128:256] = dv.astype(bf16)
            dkv_sent[d] = send(dsb.at[d - 1], drb.at[d - 1], rows[-d])
    ag_step(A, ag_a)
    g0 = unit_back(rot(dq[:, 0:TOK], co, -si) * query_scale * qg, uq0, sq0) * scale
    g1 = unit_back(rot(dq[:, TOK:], co, -si) * query_scale * qg, uq1, sq1) * scale
    Gq[y, 0:128] = g0.astype(bf16)
    Gq[y, 128:256] = g1.astype(bf16)
    ag_q = ag_start(Gq)
    ag_end(ag_a)

    def whole(B, i):
        return jnp.concatenate([B[i, j] for j in range(NY)], 1)

    stores = [(C, A), (X, Gq), (X, Gk)]

    def part(u, r):
        L, B = stores[u]
        right = jnp.concatenate([B[j] for j in range(NY)], 1)
        return dot(whole(L, zi[r % NZ]), right, 1, 1)

    zc = {}

    def zs0(u):
        t = part(u, 4).astype(bf16)
        hb[u, 0] = t[:, 0:128]
        hb[u, 1] = t[:, 128:256]
        zc[u, 0, 0] = send(hb.at[u, 0], hr.at[u, 0], zp)
        zc[u, 1, 0] = send(hb.at[u, 1], hr.at[u, 1], zm)

    def zs1(u):
        t = part(u, 3)
        zc[u, 0, 0].wait_recv()
        sb[u, 0, 0, :, 0:128] = (t[:, 0:128] + hr[u, 0].astype(f32)).astype(bf16)
        sb[u, 0, 0, :, 128:256] = t[:, 128:256].astype(bf16)
        zc[u, 0, 1] = send(sb.at[u, 0, 0], rb.at[u, 0, 0], zp)
        t = part(u, -3)
        zc[u, 1, 0].wait_recv()
        sb[u, 1, 0, :, 0:128] = t[:, 0:128].astype(bf16)
        sb[u, 1, 0, :, 128:256] = (t[:, 128:256] + hr[u, 1].astype(f32)).astype(bf16)
        zc[u, 1, 1] = send(sb.at[u, 1, 0], rb.at[u, 1, 0], zm)

    def zsn(u, n):
        for w, (sgn, dev) in enumerate(((1, zp), (-1, zm))):
            t = part(u, sgn * (4 - n))
            zc[u, w, n - 1].wait_recv()
            sb[u, w, n - 1] = (t + rb[u, w, n - 2].astype(f32)).astype(bf16)
            zc[u, w, n] = send(sb.at[u, w, n - 1], rb.at[u, w, n - 1], dev)

    def zs4(u):
        t = part(u, 0)
        zc[u, 0, 3].wait_recv()
        zc[u, 1, 3].wait_recv()
        return (t + rb[u, 0, 2].astype(f32) + rb[u, 1, 2].astype(f32)).astype(bf16)

    zs0(0)
    ag_step(Gq, ag_q)
    for d in (1, 3, 2, 4):
        dkv_sent[d].wait_recv()
    for d in (1, 3, 2, 4):
        dk = dk + drb[d - 1, 0:128].astype(f32)
        dv = dv + drb[d - 1, 128:256].astype(f32)
    gk = unit_back(rot(dk, co, -si) * kg, uk, sk) * scale
    gv = dv * scale
    Gk[y, 0:128] = gk.astype(bf16)
    Gk[y, 128:256] = gv.astype(bf16)
    ag_k = ag_start(Gk)
    inner = jnp.sum(
        g0 * proj[0:128] + g1 * proj[128:256] + gk * proj[256:384] + gv * proj[384:512], 0, keepdims=True
    )
    inn[c] = jnp.broadcast_to(inner, (8, TOK))
    in_sent = [send(inn.at[c], inn.at[c], dev) for dev in cols]
    zs1(0)
    ag_end(ag_q)
    zs0(1)
    ag_step(Gk, ag_k)
    zsn(0, 2)
    zs1(1)
    ag_end(ag_k)

    def share(i, j):
        g = jnp.concatenate([Gq[j], Gk[j]], 0)
        return dot(Wp[i], g, 1, 0)

    nc = {}
    for r in (2, 1, 3, 0):
        for j in range(NY):
            nb[r, j] = share(xi[r] * NK + ko, j).astype(bf16)
        nc[r] = send(nb.at[r], nr.at[r], sib)
    zs0(2)
    zsn(0, 3)
    nc[2].wait_recv()
    for j in range(NY):
        mh[j] = (share(xi[2] * NK + k, j) + nr[2, j].astype(f32)).astype(bf16)
    xf = send(mh.at[pl.ds(0, 2)], mrh.at[0], xp)
    xb = send(mh.at[pl.ds(2, 2)], mrh.at[1], xm)
    zsn(1, 2)
    zs1(2)
    nc[1].wait_recv()
    nc[3].wait_recv()
    mid = {}
    for w, r in enumerate((1, 3)):
        (xf, xb)[w].wait_recv()
        for j in range(NY):
            t = share(xi[r] * NK + k, j) + nr[r, j].astype(f32)
            if j // 2 == w:
                t = t + mrh[w, j % 2].astype(f32)
            mb[w, j] = t.astype(bf16)
        mid[w] = send(mb.at[w], mr.at[w], (xp, xm)[w])
    g_wo[...] = zs4(0)
    zsn(1, 3)
    zsn(2, 2)
    nc[0].wait_recv()
    mid[0].wait_recv()
    mid[1].wait_recv()
    for j in range(NY):
        t = share(xi[0] * NK + k, j) + nr[0, j].astype(f32)
        ds_[j] = (t + mr[0, j].astype(f32) + mr[1, j].astype(f32)).astype(bf16)
    dr_[y] = ds_[y]
    back = [send(ds_.at[yi[e]], dr_.at[y], {"y": yi[e]}) for e in (2, 1, 3)]
    zsn(2, 3)
    g_wq[...] = zs4(1)
    for s in in_sent:
        s.wait_recv()
    in_total = inn[0, 0:1]
    for i in range(1, NC):
        in_total = in_total + inn[i, 0:1]
    factor = scale * in_total / D
    for s in back:
        s.wait_recv()
    for j in range(NY):
        here = slice(j * FR, (j + 1) * FR)
        dn[here] = dr_[j].astype(f32) * gain[here] - raw[here] * factor
    g_in[...] = dot(eye(TOK), dn[...].astype(bf16), 1, 1).astype(bf16)
    last = zs4(2)
    g_wk[...] = last[:, 0:128]
    g_wv[...] = last[:, 128:256]
    for s in started:
        s.wait_send()


def tables(row):
    half = HD // 2
    positions = (row * TOK + jnp.arange(TOK, dtype=jnp.int32)).astype(f32)
    frequency = 10000.0 ** (-(2.0 * jnp.arange(half, dtype=f32)) / HD)
    angles = frequency[:, None] * positions[None, :]
    return jnp.cos(angles), jnp.sin(angles)


def per_device(tokens, input_gain, q_gain, k_gain, wq, wk, wv, wo, upstream, doc_ids, doc_labels):
    row = lax.axis_index("z") * NY + lax.axis_index("y")
    cos_t, sin_t = tables(row)
    V = pltpu.VMEM
    piece = (FR, TOK)
    scratch = [
        V((NY,) + piece, bf16), V((NY,) + piece, bf16),
        V((NC, NY) + piece, bf16), V((NC, NY) + piece, bf16),
        V((NZ, FR, 512), bf16), V((NZ, FR, 256), bf16),
        V((NC, 8, TOK), f32), V((NC, 8, TOK), f32), V((NY * FR, TOK), f32),
        V((3, 512, TOK), bf16), V((2, 512, TOK), bf16), V((2, 256, TOK), bf16),
        V((3, 256, TOK), bf16), V((2, 256, TOK), bf16), V((2, 128, TOK), bf16),
        V((5, 256, TOK), bf16), V((5, TOK, 2 * TOK), f32),
        V((4, 256, TOK), bf16), V((4, 256, TOK), bf16),
        V((NY, 256, TOK), bf16), V((NY, 256, TOK), bf16), V((NY, 256, TOK), bf16),
        V((3, 2, FR, 128), bf16), V((3, 2, FR, 128), bf16),
        V((3, 2, 3, FR, 256), bf16), V((3, 2, 3, FR, 256), bf16),
        V((NX, NY) + piece, bf16), V((NX, NY) + piece, bf16),
        V((NY,) + piece, bf16), V((2, 2) + piece, bf16),
        V((2, NY) + piece, bf16), V((2, NY) + piece, bf16),
        V((NY,) + piece, bf16), V((NY,) + piece, bf16), V((NY * FR, TOK), f32),
        pltpu.SemaphoreType.DMA((NSEM,)), pltpu.SemaphoreType.DMA((NSEM,)),
    ]
    vm = pl.BlockSpec(memory_space=pltpu.VMEM)
    out = [
        jax.ShapeDtypeStruct((TOK, NY * FR), bf16),
        jax.ShapeDtypeStruct((FR, 256), bf16),
        jax.ShapeDtypeStruct((FR, 128), bf16),
        jax.ShapeDtypeStruct((FR, 128), bf16),
        jax.ShapeDtypeStruct((FR, 256), bf16),
    ]
    return pl.pallas_call(
        kernel,
        out_shape=out,
        in_specs=[vm] * 12 + [pl.BlockSpec(memory_space=pltpu.SMEM)],
        out_specs=[vm] * 5,
        scratch_shapes=scratch,
        compiler_params=pltpu.CompilerParams(
            collective_id=0, has_side_effects=True, vmem_limit_bytes=60 * 1024 * 1024
        ),
    )(
        tokens, upstream, input_gain[:, None], q_gain[:, None], k_gain[:, None], wq, wk, wv, wo,
        cos_t, sin_t, doc_ids.reshape(NZ * NY, TOK), doc_labels,
    )


def solution(mesh):
    fine = Mesh(mesh.devices.reshape(NZ, NY, NX, NK), ("z", "y", "x", "k"))
    rc = P(("z", "y"), ("x", "k"))
    return jax.shard_map(
        per_device,
        mesh=fine,
        in_specs=(rc, P(("x", "k")), P(), P(), rc, rc, rc, rc, rc, P(), P()),
        out_specs=(rc,) * 5,
        check_vma=False,
    )
```

```python
import math

import jax
import jax.numpy as jnp
from jax import lax
from jax.experimental import pallas as pl
from jax.experimental.pallas import tpu as pltpu
from jax.sharding import Mesh
from jax.sharding import PartitionSpec as P

D = 5376
HD = 128
WIN = 1024
NZ, NY, NX, NK = 8, 4, 4, 2
NC = NX * NK
TOK = 256
FR = 168
NDOC = 8
NSEM = 256
epsilon = 1e-06
query_scale = 168.0 ** (-0.5)
f32 = jnp.float32
bf16 = jnp.bfloat16
MESH = pl.DeviceIdType.MESH


def dot(a, b, ca, cb):
    return lax.dot_general(a, b, (((ca,), (cb,)), ((), ())), preferred_element_type=f32)


def rot(v, c, s):
    a, b = v[: HD // 2], v[HD // 2 :]
    return jnp.concatenate([a * c - b * s, b * c + a * s], 0)


def unit(p):
    sc = lax.rsqrt(jnp.mean(p * p, 0, keepdims=True) + epsilon)
    return p * sc, sc


def unit_back(w, u, sc):
    return sc * (w - u * jnp.mean(w * u, 0, keepdims=True))


def column(v):
    n = v.shape[1]
    parts = []
    for i in range(0, n, 128):
        w = min(128, n - i)
        same = lax.broadcasted_iota(jnp.int32, (w, w), 0) == lax.broadcasted_iota(jnp.int32, (w, w), 1)
        parts.append(jnp.sum(jnp.where(same, v[:, i : i + w], 0.0), 1, keepdims=True))
    return jnp.concatenate(parts, 0) if len(parts) > 1 else parts[0]


def kernel(
    tokens, upstream, gain, q_gain, k_gain, wq, wk, wv, wo, docs_in, labels,
    g_in, g_wq, g_wk, g_wv, g_wo,
    tok, ups, g_row, qg_row, kg_row, docs,
    xsrc, csrc, X, C, Wp, Wo, ssq, inn, gcol, cs,
    pq, pr, prh,
    KV, ex, dsb, drb, A, Gq, Gk,
    hb, hr, sb, rb,
    nb, nr, mh, mrh, mb, mr, ds_, dr_,
    sem_l, sem_s, sem_r,
):
    z, y, x, k = (lax.axis_index(n) for n in ("z", "y", "x", "k"))
    c = x * NK + k
    row = z * NY + y
    zi = [lax.rem(z + r, NZ) for r in range(NZ)]
    yi = [lax.rem(y + r, NY) for r in range(NY)]
    xi = [lax.rem(x + r, NX) for r in range(NX)]
    ko = 1 - k
    zp, zm = {"z": zi[1]}, {"z": zi[NZ - 1]}
    yp, ym = {"y": yi[1]}, {"y": yi[NY - 1]}
    xp, xm = {"x": xi[1]}, {"x": xi[NX - 1]}
    sib = {"k": ko}
    cols = []
    for d in range(1, NC):
        cc = lax.rem(c + d, NC)
        cols.append({"x": cc // NK, "k": lax.rem(cc, NK)})

    barrier = pltpu.get_barrier_semaphore()
    peers = [zp, zm, yp, ym, {"y": yi[2]}] + cols
    for dev in peers:
        pl.semaphore_signal(barrier, inc=1, device_id=dev, device_id_type=MESH)

    loads = []
    for n, (src, dst) in enumerate((
        (wq, Wp.at[z, :, pl.ds(0, 256)]), (wk, Wp.at[z, :, pl.ds(256, 128)]), (wv, Wp.at[z, :, pl.ds(384, 128)]),
        (tokens, tok), (gain, g_row), (docs_in, docs), (upstream, ups), (wo, Wo.at[z]), (q_gain, qg_row), (k_gain, kg_row),
    )):
        loads.append(pltpu.make_async_copy(src, dst, sem_l.at[n]))
        loads[-1].start()

    count = [0]
    started = []

    def make(src, dst, dev, i):
        return pltpu.make_async_remote_copy(
            src_ref=src, dst_ref=dst, send_sem=sem_s.at[i], recv_sem=sem_r.at[i],
            device_id=dev, device_id_type=MESH,
        )

    def send(src, dst, dev):
        i = count[0]
        count[0] += 1
        copy = make(src, dst, dev, i)
        copy.start()
        started.append(copy)
        return copy

    def ring_start(W):
        return [send(W.at[z], W.at[z], zp)], [send(W.at[z], W.at[z], zm)]

    def ring_step(W, fwd, bwd, half):
        s = len(fwd)
        zf, zb = zi[NZ - s], zi[s]
        fwd[-1].wait_recv()
        if s < 3:
            fwd.append(send(W.at[zf], W.at[zf], zp))
        elif s == 3:
            fwd.append(send(W.at[zf, :, pl.ds(0, half)], W.at[zf, :, pl.ds(0, half)], zp))
        bwd[-1].wait_recv()
        if s < 3:
            bwd.append(send(W.at[zb], W.at[zb], zm))
        elif s == 3:
            bwd.append(send(W.at[zb, :, pl.ds(half, half)], W.at[zb, :, pl.ds(half, half)], zm))

    def exchange(src, Y):
        out = {}
        for e in (1, 3, 2):
            out[e] = send(src.at[yi[e]], Y.at[c, y], {"y": yi[e]})
        Y[c, y] = src[yi[0]]
        return out

    def spread(Y, e, far):
        ref = Y.at[c, yi[e]]
        far["p", e] = send(ref, ref, xp)
        far["m", e] = send(ref, ref, xm)
        far["s", 0, e] = send(ref, ref, sib)

    def onward(Y, e, far):
        left = Y.at[xi[NX - 1] * NK + k, yi[e]]
        right = Y.at[xi[1] * NK + k, yi[e]]
        far["p", e].wait_recv()
        if e in (0, 1):
            far["f", e] = send(left, left, xp)
        far["s", 1, e] = send(left, left, sib)
        far["m", e].wait_recv()
        if e in (2, 3):
            far["f", e] = send(right, right, xm)
        far["s", 2, e] = send(right, right, sib)

    def across(Y, e, far):
        ref = Y.at[xi[2] * NK + k, yi[e]]
        far["f", e].wait_recv()
        far["s", 3, e] = send(ref, ref, sib)

    def gathered(far):
        for i in range(4):
            for e in range(NY):
                far["s", i, e].wait_recv()

    for n in (3, 4):
        loads[n].wait()
    gcol[...] = column(g_row[...])
    x32 = tok[...].astype(f32)
    ssq[c] = jnp.broadcast_to(jnp.sum(x32 * x32, 0, keepdims=True), (8, TOK))
    for i in range(NY):
        here = slice(i * FR, (i + 1) * FR)
        xsrc[i] = (tok[here].astype(f32) * gcol[here]).astype(bf16)
    for n in (0, 1, 2):
        loads[n].wait()
    pl.semaphore_wait(barrier, len(peers))

    a2x = exchange(xsrc, X)
    ring_p = ring_start(Wp)
    fx, fc = {}, {}
    spread(X, 0, fx)
    sq_sent = [send(ssq.at[c], ssq.at[c], dev) for dev in cols]

    for n in (5, 6, 7, 8, 9):
        loads[n].wait()
    own_docs = jnp.concatenate([docs[pl.ds(2 * row, 1), :], docs[pl.ds(2 * row + 1, 1), :]], 1).astype(f32)
    all_docs = docs[...].astype(f32)
    sign = jnp.ones((1, TOK), f32)
    start = jnp.zeros((1, TOK), f32)
    for d in range(NDOC):
        member = (own_docs == d).astype(f32)
        sign = sign - 2.0 * member * labels[d].astype(f32)
        start = start + member * jnp.sum(
            jnp.sum((all_docs < d).astype(f32), 0, keepdims=True), 1, keepdims=True
        )
    lane = lax.broadcasted_iota(jnp.int32, (1, TOK), 1).astype(f32)
    low = jnp.maximum(start - (row * TOK).astype(f32), lane - (WIN - 1.0))
    for i in range(NY):
        csrc[i] = (ups[i * FR : (i + 1) * FR].astype(f32) * sign).astype(bf16)

    for e in (1, 3):
        a2x[4 - e].wait_recv()
        spread(X, e, fx)
    a2c = exchange(csrc, C)
    onward(X, 0, fx)
    a2x[2].wait_recv()
    spread(X, 2, fx)
    ring_step(Wp, *ring_p, 256)
    half = lax.broadcasted_iota(jnp.int32, (HD // 2, TOK), 0).astype(f32)
    place = lax.broadcasted_iota(jnp.int32, (HD // 2, TOK), 1) + row * TOK
    angles = place.astype(f32) * jnp.exp(half * (-2.0 * math.log(10000.0) / HD))
    cs[0] = jnp.cos(angles)
    cs[1] = jnp.sin(angles)
    onward(X, 1, fx)
    onward(X, 3, fx)
    ring_step(Wp, *ring_p, 256)
    onward(X, 2, fx)
    for e in (1, 3, 2):
        a2c[4 - e].wait_recv()
    for e in (0, 1, 3, 2):
        spread(C, e, fc)
    for e in (0, 1, 3):
        across(X, e, fx)
    ring_step(Wp, *ring_p, 256)
    ring_o = ring_start(Wo)
    across(X, 2, fx)
    gathered(fx)
    onward(C, 0, fc)
    ring_step(Wp, *ring_p, 256)

    def partial(u, e):
        total = None
        for i in range(NC):
            if u < 2:
                t = dot(Wp[i, :, u * 256 : u * 256 + 256], X[i, yi[e]], 0, 0)
            else:
                t = dot(Wo[i], C[i, yi[e]], 0, 0)
            total = t if total is None else total + t
        return total

    def reduce_far(u):
        pq[u, 0] = partial(u, 2).astype(bf16)
        return (
            send(pq.at[u, 0, pl.ds(0, 128)], prh.at[u, 0], yp),
            send(pq.at[u, 0, pl.ds(128, 128)], prh.at[u, 1], ym),
        )

    def reduce_near(u, sent):
        t1 = partial(u, 1)
        t3 = partial(u, 3)
        sent[0].wait_recv()
        pq[u, 1, 0:128] = (t1[0:128] + prh[u, 0].astype(f32)).astype(bf16)
        pq[u, 1, 128:256] = t1[128:256].astype(bf16)
        a = send(pq.at[u, 1], pr.at[u, 0], yp)
        sent[1].wait_recv()
        pq[u, 2, 0:128] = t3[0:128].astype(bf16)
        pq[u, 2, 128:256] = (t3[128:256] + prh[u, 1].astype(f32)).astype(bf16)
        b = send(pq.at[u, 2], pr.at[u, 1], ym)
        return a, b

    def reduced(u, own, sent):
        sent[0].wait_recv()
        sent[1].wait_recv()
        return own + pr[u, 0].astype(f32) + pr[u, 1].astype(f32)

    far_k = reduce_far(1)
    far_q = reduce_far(0)
    near_k = reduce_near(1, far_k)
    ring_step(Wo, *ring_o, 128)
    onward(C, 1, fc)
    near_q = reduce_near(0, far_q)
    own_k = partial(1, 0)
    ring_step(Wo, *ring_o, 128)
    onward(C, 3, fc)
    for s in sq_sent:
        s.wait_recv()
    total_sq = ssq[0, 0:1]
    for i in range(1, NC):
        total_sq = total_sq + ssq[i, 0:1]
    scale = lax.rsqrt(total_sq / D + epsilon)
    co, si = cs[0], cs[1]
    qg, kg = column(qg_row[...]), column(kg_row[...])
    kv_proj = reduced(1, own_k, near_k) * scale
    uk, sk = unit(kv_proj[0:128])
    KV[0, 0:128] = rot(uk * kg, co, si).astype(bf16)
    KV[0, 128:256] = kv_proj[128:256].astype(bf16)
    kv_sent = {4: send(KV.at[0], KV.at[4], zp)}
    later = []
    for e in (1, 3, 2):
        i = count[0]
        count[0] += 1
        first = make(KV.at[0], KV.at[e], {"y": yi[e]}, i)
        second = make(KV.at[4], KV.at[e], {"y": yi[e]}, i)
        pl.when(y + e < NY)(first.start)
        later.append((e, second))
        kv_sent[e] = first
        started.append(first)
    onward(C, 2, fc)
    ring_step(Wo, *ring_o, 128)
    across(C, 0, fc)
    own_q = partial(0, 0)
    q_proj = reduced(0, own_q, near_q) * scale
    kv_sent[4].wait_recv()
    for e, second in later:
        pl.when(y + e >= NY)(second.start)
    across(C, 1, fc)
    across(C, 3, fc)
    ring_step(Wo, *ring_o, 128)
    uq0, sq0 = unit(q_proj[0:128])
    uq1, sq1 = unit(q_proj[128:256])
    q = jnp.concatenate([rot(uq0 * qg, co, si), rot(uq1 * qg, co, si)], 1) * query_scale
    q = q.astype(bf16)
    across(C, 2, fc)
    gathered(fc)
    far_o = reduce_far(2)

    low2 = jnp.concatenate([low, low], 1)
    at2 = jnp.concatenate([lane, lane], 1)
    below = lax.broadcasted_iota(jnp.int32, (TOK, 2 * TOK), 0).astype(f32)

    def scores(d, total, attn):
        s = dot(KV[d, 0:128], q, 0, 0)
        ok = below >= low2 + d * TOK
        if d == 0:
            ok = ok & (below <= at2)
        e = jnp.where(ok, jnp.exp(s), 0.0)
        ex[d] = e
        total = total + jnp.sum(e, 0, keepdims=True)
        return total, attn + dot(KV[d, 128:256], e.astype(bf16), 1, 0)

    total, attn = scores(0, jnp.zeros((1, 2 * TOK), f32), jnp.zeros((HD, 2 * TOK), f32))
    near_o = reduce_near(2, far_o)
    own_o = partial(2, 0)
    for d in (4, 1, 3, 2):
        if d < 4:
            kv_sent[d].wait_recv()
        total, attn = scores(d, total, attn)
    inv = 1.0 / total
    attn = attn * inv
    A[y, 0:128] = attn[:, 0:TOK].astype(bf16)
    A[y, 128:256] = attn[:, TOK:].astype(bf16)

    def ag_start(B):
        return [send(B.at[y], B.at[y], yp), send(B.at[y], B.at[y], ym)]

    def ag_step(B, s):
        s[0].wait_recv()
        low_half = B.at[yi[3], pl.ds(0, 128)]
        s.append(send(low_half, low_half, yp))
        s[1].wait_recv()
        high_half = B.at[yi[1], pl.ds(128, 128)]
        s.append(send(high_half, high_half, ym))

    def ag_end(s):
        s[2].wait_recv()
        s[3].wait_recv()

    da = reduced(2, own_o, near_o)
    ag_a = ag_start(A)
    da = jnp.concatenate([da[0:128], da[128:256]], 1).astype(bf16)
    delta = jnp.sum(attn * da.astype(f32), 0, keepdims=True)
    dq = jnp.zeros((HD, 2 * TOK), f32)
    dkv_sent = {}
    for d in (2, 1, 3, 4, 0):
        p = ex[d] * inv
        dp = dot(KV[d, 128:256], da, 0, 0)
        ds = (p * (dp - delta)).astype(bf16)
        dq = dq + dot(KV[d, 0:128], ds, 1, 0)
        dk = dot(q, ds, 1, 1)
        dv = dot(da, p.astype(bf16), 1, 1)
        if d in (1, 2, 3):
            dsb[d - 1, 0:128] = dk.astype(bf16)
            dsb[d - 1, 128:256] = dv.astype(bf16)
            dkv_sent[d] = send(dsb.at[d - 1], drb.at[d - 1], {"y": yi[NY - d]})
        if d == 4:
            dk4, dv4 = dk, dv
    g0 = unit_back(rot(dq[:, 0:TOK], co, -si) * query_scale * qg, uq0, sq0) * scale
    g1 = unit_back(rot(dq[:, TOK:], co, -si) * query_scale * qg, uq1, sq1) * scale
    Gq[y, 0:128] = g0.astype(bf16)
    Gq[y, 128:256] = g1.astype(bf16)
    ag_step(A, ag_a)
    for d in (1, 3, 2):
        dkv_sent[d].wait_recv()
    for d in (1, 2, 3):
        mine = jnp.where(y + d < NY, 1.0, 0.0)
        gk, gv = drb[d - 1, 0:128].astype(f32), drb[d - 1, 128:256].astype(f32)
        dk, dv = dk + gk * mine, dv + gv * mine
        dk4, dv4 = dk4 + gk * (1.0 - mine), dv4 + gv * (1.0 - mine)
    dsb[3, 0:128] = dk4.astype(bf16)
    dsb[3, 128:256] = dv4.astype(bf16)
    dkv_sent[4] = send(dsb.at[3], drb.at[3], zm)
    ag_q = ag_start(Gq)
    ag_end(ag_a)

    stores = [(C, A), (X, Gq), (X, Gk)]

    def part(u, r):
        L, B = stores[u]
        i = zi[r % NZ]
        left = jnp.concatenate([L[i, j] for j in range(NY)], 1)
        right = jnp.concatenate([B[j] for j in range(NY)], 1)
        return dot(left, right, 1, 1)

    zc = {}

    def zs0(u):
        t = part(u, 4).astype(bf16)
        hb[u, 0] = t[:, 0:128]
        hb[u, 1] = t[:, 128:256]
        zc[u, 0, 0] = send(hb.at[u, 0], hr.at[u, 0], zp)
        zc[u, 1, 0] = send(hb.at[u, 1], hr.at[u, 1], zm)

    def zs1(u):
        t = part(u, 3)
        t3 = part(u, -3)
        zc[u, 0, 0].wait_recv()
        sb[u, 0, 0, :, 0:128] = (t[:, 0:128] + hr[u, 0].astype(f32)).astype(bf16)
        sb[u, 0, 0, :, 128:256] = t[:, 128:256].astype(bf16)
        zc[u, 0, 1] = send(sb.at[u, 0, 0], rb.at[u, 0, 0], zp)
        zc[u, 1, 0].wait_recv()
        sb[u, 1, 0, :, 0:128] = t3[:, 0:128].astype(bf16)
        sb[u, 1, 0, :, 128:256] = (t3[:, 128:256] + hr[u, 1].astype(f32)).astype(bf16)
        zc[u, 1, 1] = send(sb.at[u, 1, 0], rb.at[u, 1, 0], zm)

    def zsn(u, n):
        t = [part(u, 4 - n), part(u, n - 4)]
        for w, dev in enumerate((zp, zm)):
            zc[u, w, n - 1].wait_recv()
            sb[u, w, n - 1] = (t[w] + rb[u, w, n - 2].astype(f32)).astype(bf16)
            zc[u, w, n] = send(sb.at[u, w, n - 1], rb.at[u, w, n - 1], dev)

    def zs4(u):
        t = part(u, 0)
        zc[u, 0, 3].wait_recv()
        zc[u, 1, 3].wait_recv()
        return (t + rb[u, 0, 2].astype(f32) + rb[u, 1, 2].astype(f32)).astype(bf16)

    zs0(0)
    dkv_sent[4].wait_recv()
    dk = dk + drb[3, 0:128].astype(f32)
    dv = dv + drb[3, 128:256].astype(f32)
    gk = unit_back(rot(dk, co, -si) * kg, uk, sk) * scale
    gv = dv * scale
    Gk[y, 0:128] = gk.astype(bf16)
    Gk[y, 128:256] = gv.astype(bf16)
    ag_k = ag_start(Gk)
    inner = jnp.sum(
        g0 * q_proj[0:128] + g1 * q_proj[128:256] + gk * kv_proj[0:128] + gv * kv_proj[128:256], 0, keepdims=True
    )
    inn[c] = jnp.broadcast_to(inner, (8, TOK))
    in_sent = [send(inn.at[c], inn.at[c], dev) for dev in cols]
    ag_step(Gq, ag_q)
    zs1(0)
    ag_end(ag_q)
    zs0(1)
    ag_step(Gk, ag_k)
    zsn(0, 2)
    zs1(1)
    ag_end(ag_k)

    def share(i, j):
        j = yi[j]
        g = jnp.concatenate([Gq[j], Gk[j]], 0)
        return dot(Wp[i], g, 1, 0)

    nc = {}

    def to_sibling(r):
        for j in range(NY):
            nb[r, j] = share(xi[r] * NK + ko, j).astype(bf16)
        nc[r] = send(nb.at[r], nr.at[r], sib)

    to_sibling(2)
    to_sibling(1)
    t2 = [share(xi[2] * NK + k, e) for e in range(NY)]
    nc[2].wait_recv()
    xc = {}
    for e in (1, 2, 0, 3):
        mh[e] = (t2[e] + nr[2, e].astype(f32)).astype(bf16)
        xc[e] = send(mh.at[e], mrh.at[e], xp if e < 2 else xm)
    to_sibling(3)
    zs0(2)
    to_sibling(0)
    zsn(0, 3)
    nc[1].wait_recv()
    nc[3].wait_recv()
    mid = {}

    def middle(w, e):
        r = (1, 3)[w]
        t = share(xi[r] * NK + k, e) + nr[r, e].astype(f32)
        if e // 2 == w:
            xc[e].wait_recv()
            t = t + mrh[e].astype(f32)
        mb[w, e] = t.astype(bf16)
        mid[w, e] = send(mb.at[w, e], mr.at[w, e], (xp, xm)[w])

    middle(0, 2)
    middle(1, 1)
    middle(0, 1)
    middle(1, 2)
    zsn(1, 2)
    zs1(2)
    middle(0, 3)
    middle(1, 0)
    middle(0, 0)
    middle(1, 3)
    g_wo[...] = zs4(0)
    zsn(1, 3)
    zsn(2, 2)
    nc[0].wait_recv()
    back = []
    for e in (2, 1, 3, 0):
        t = share(xi[0] * NK + k, e) + nr[0, e].astype(f32)
        mid[0, e].wait_recv()
        mid[1, e].wait_recv()
        t = (t + mr[0, e].astype(f32) + mr[1, e].astype(f32)).astype(bf16)
        if e:
            ds_[e] = t
            back.append(send(ds_.at[e], dr_.at[y], {"y": yi[e]}))
        else:
            dr_[y] = t
        if e == 2:
            zsn(2, 3)
    g_wq[...] = zs4(1)
    for s in in_sent:
        s.wait_recv()
    in_total = inn[0, 0:1]
    for i in range(1, NC):
        in_total = in_total + inn[i, 0:1]
    factor = scale * in_total / D
    last = zs4(2)
    g_wk[...] = last[:, 0:128]
    g_wv[...] = last[:, 128:256]
    for s in back:
        s.wait_recv()
    for j in range(NY):
        here = slice(j * FR, (j + 1) * FR)
        g_in[here] = (dr_[j].astype(f32) * gcol[here] - tok[here].astype(f32) * factor).astype(bf16)
    for s in started:
        s.wait_send()


def hand_over(*refs):
    n = len(refs) // 2
    copies = [pltpu.make_async_copy(refs[i], refs[n + i], refs[-1].at[i]) for i in range(n)]
    for copy in copies:
        copy.start()
    for copy in copies:
        copy.wait()


def per_device(tokens, input_gain, q_gain, k_gain, wq, wk, wv, wo, upstream, doc_ids, doc_labels):
    V = pltpu.VMEM
    piece = (FR, TOK)
    scratch = [
        V((NY * FR, TOK), bf16), V((NY * FR, TOK), bf16), V((1, NY * FR), f32), V((1, HD), f32), V((1, HD), f32),
        V((NZ * NY * TOK // 128, 128), jnp.int32),
        V((NY,) + piece, bf16), V((NY,) + piece, bf16),
        V((NC, NY) + piece, bf16), V((NC, NY) + piece, bf16),
        V((NZ, FR, 512), bf16), V((NZ, FR, 256), bf16),
        V((NC, 8, TOK), f32), V((NC, 8, TOK), f32), V((NY * FR, 1), f32), V((2, HD // 2, TOK), f32),
        V((3, 3, 256, TOK), bf16), V((3, 2, 256, TOK), bf16), V((3, 2, 128, TOK), bf16),
        V((5, 256, TOK), bf16), V((5, TOK, 2 * TOK), f32),
        V((4, 256, TOK), bf16), V((4, 256, TOK), bf16),
        V((NY, 256, TOK), bf16), V((NY, 256, TOK), bf16), V((NY, 256, TOK), bf16),
        V((3, 2, FR, 128), bf16), V((3, 2, FR, 128), bf16),
        V((3, 2, 3, FR, 256), bf16), V((3, 2, 3, FR, 256), bf16),
        V((NX, NY) + piece, bf16), V((NX, NY) + piece, bf16),
        V((NY,) + piece, bf16), V((NY,) + piece, bf16),
        V((2, NY) + piece, bf16), V((2, NY) + piece, bf16),
        V((NY,) + piece, bf16), V((NY,) + piece, bf16),
        pltpu.SemaphoreType.DMA((10,)), pltpu.SemaphoreType.DMA((NSEM,)), pltpu.SemaphoreType.DMA((NSEM,)),
    ]
    vm = pl.BlockSpec(memory_space=pltpu.VMEM)
    hbm = pl.BlockSpec(memory_space=pl.ANY)
    out = [
        jax.ShapeDtypeStruct((NY * FR, TOK), bf16),
        jax.ShapeDtypeStruct((FR, 256), bf16),
        jax.ShapeDtypeStruct((FR, 128), bf16),
        jax.ShapeDtypeStruct((FR, 128), bf16),
        jax.ShapeDtypeStruct((FR, 256), bf16),
    ]
    results = pl.pallas_call(
        kernel,
        out_shape=out,
        in_specs=[hbm] * 10 + [pl.BlockSpec(memory_space=pltpu.SMEM)],
        out_specs=[vm] * 5,
        scratch_shapes=scratch,
        compiler_params=pltpu.CompilerParams(
            collective_id=0, has_side_effects=True, vmem_limit_bytes=60 * 1024 * 1024
        ),
    )(
        tokens.T, upstream.T, input_gain[None, :], q_gain[None, :], k_gain[None, :], wq, wk, wv, wo,
        doc_ids.reshape(-1, 128), doc_labels,
    )
    results = pl.pallas_call(
        hand_over,
        out_shape=out,
        in_specs=[hbm] * 5,
        out_specs=[hbm] * 5,
        scratch_shapes=[pltpu.SemaphoreType.DMA((5,))],
        compiler_params=pltpu.CompilerParams(vmem_limit_bytes=60 * 1024 * 1024),
    )(*results)
    return (results[0].T, *results[1:])


def solution(mesh):
    fine = Mesh(mesh.devices.reshape(NZ, NY, NX, NK), ("z", "y", "x", "k"))
    rc = P(("z", "y"), ("x", "k"))
    return jax.shard_map(
        per_device,
        mesh=fine,
        in_specs=(rc, P(("x", "k")), P(), P(), rc, rc, rc, rc, rc, P(), P()),
        out_specs=(rc,) * 5,
        check_vma=False,
    )
```

```python
import math

import jax
import jax.numpy as jnp
from jax import lax
from jax.experimental import pallas as pl
from jax.experimental.pallas import tpu as pltpu
from jax.sharding import Mesh
from jax.sharding import PartitionSpec as P

D = 5376
HD = 128
WIN = 1024
NZ, NY, NX, NK = 8, 4, 4, 2
NC = NX * NK
TOK = 256
FR = 168
NDOC = 8
NSEM = 256
epsilon = 1e-06
query_scale = 168.0 ** (-0.5)
f32 = jnp.float32
bf16 = jnp.bfloat16
MESH = pl.DeviceIdType.MESH


def dot(a, b, ca, cb):
    return lax.dot_general(a, b, (((ca,), (cb,)), ((), ())), preferred_element_type=f32)


def rot(v, c, s):
    a, b = v[: HD // 2], v[HD // 2 :]
    return jnp.concatenate([a * c - b * s, b * c + a * s], 0)


def unit(p):
    sc = lax.rsqrt(jnp.mean(p * p, 0, keepdims=True) + epsilon)
    return p * sc, sc


def unit_back(w, u, sc):
    return sc * (w - u * jnp.mean(w * u, 0, keepdims=True))


def column(v):
    n = v.shape[1]
    parts = []
    for i in range(0, n, 128):
        w = min(128, n - i)
        same = lax.broadcasted_iota(jnp.int32, (w, w), 0) == lax.broadcasted_iota(jnp.int32, (w, w), 1)
        parts.append(jnp.sum(jnp.where(same, v[:, i : i + w], 0.0), 1, keepdims=True))
    return jnp.concatenate(parts, 0) if len(parts) > 1 else parts[0]


def kernel(
    tokens, upstream, gain, q_gain, k_gain, wq, wk, wv, wo, docs_in, labels,
    g_in, g_wq, g_wk, g_wv, g_wo,
    tok, ups, g_row, qg_row, kg_row, docs,
    xsrc, csrc, X, C, Wp, Wo, ssq, inn, gcol, cs,
    pq, pr, prh,
    KV, ex, dsb, drb, A, Gq, Gk,
    hb, hr, sb, rb,
    nb, nr, mh, mrh, mb, mr, ds_, dr_,
    sem_l, sem_s, sem_r,
):
    z, y, x, k = (lax.axis_index(n) for n in ("z", "y", "x", "k"))
    c = x * NK + k
    row = z * NY + y
    zi = [lax.rem(z + r, NZ) for r in range(NZ)]
    yi = [lax.rem(y + r, NY) for r in range(NY)]
    xi = [lax.rem(x + r, NX) for r in range(NX)]
    ko = 1 - k
    zp, zm = {"z": zi[1]}, {"z": zi[NZ - 1]}
    yp, ym = {"y": yi[1]}, {"y": yi[NY - 1]}
    xp, xm = {"x": xi[1]}, {"x": xi[NX - 1]}
    sib = {"k": ko}
    cols = []
    for d in range(1, NC):
        cc = lax.rem(c + d, NC)
        cols.append({"x": cc // NK, "k": lax.rem(cc, NK)})

    barrier = pltpu.get_barrier_semaphore()
    peers = [zp, zm, yp, ym, {"y": yi[2]}] + cols
    for dev in peers:
        pl.semaphore_signal(barrier, inc=1, device_id=dev, device_id_type=MESH)

    loads = []
    for n, (src, dst) in enumerate((
        (wq, Wp.at[z, :, pl.ds(0, 256)]), (wk, Wp.at[z, :, pl.ds(256, 128)]), (wv, Wp.at[z, :, pl.ds(384, 128)]),
        (tokens, tok), (gain, g_row), (docs_in, docs), (upstream, ups), (wo, Wo.at[z]), (q_gain, qg_row), (k_gain, kg_row),
    )):
        loads.append(pltpu.make_async_copy(src, dst, sem_l.at[n]))
        loads[-1].start()

    count = [0]
    started = []

    def make(src, dst, dev, i):
        return pltpu.make_async_remote_copy(
            src_ref=src, dst_ref=dst, send_sem=sem_s.at[i], recv_sem=sem_r.at[i],
            device_id=dev, device_id_type=MESH,
        )

    def send(src, dst, dev):
        i = count[0]
        count[0] += 1
        copy = make(src, dst, dev, i)
        copy.start()
        started.append(copy)
        return copy

    def ring_start(W):
        return [send(W.at[z], W.at[z], zp)], [send(W.at[z], W.at[z], zm)]

    def ring_step(W, fwd, bwd, half):
        s = len(fwd)
        zf, zb = zi[NZ - s], zi[s]
        fwd[-1].wait_recv()
        if s < 3:
            fwd.append(send(W.at[zf], W.at[zf], zp))
        elif s == 3:
            fwd.append(send(W.at[zf, :, pl.ds(0, half)], W.at[zf, :, pl.ds(0, half)], zp))
        bwd[-1].wait_recv()
        if s < 3:
            bwd.append(send(W.at[zb], W.at[zb], zm))
        elif s == 3:
            bwd.append(send(W.at[zb, :, pl.ds(half, half)], W.at[zb, :, pl.ds(half, half)], zm))

    def exchange(src, Y):
        out = {}
        for e in (1, 3, 2):
            out[e] = send(src.at[yi[e]], Y.at[c, y], {"y": yi[e]})
        Y[c, y] = src[yi[0]]
        return out

    def spread(Y, e, far):
        ref = Y.at[c, yi[e]]
        far["p", e] = send(ref, ref, xp)
        far["m", e] = send(ref, ref, xm)
        far["s", 0, e] = send(ref, ref, sib)

    def onward(Y, e, far):
        left = Y.at[xi[NX - 1] * NK + k, yi[e]]
        right = Y.at[xi[1] * NK + k, yi[e]]
        far["p", e].wait_recv()
        if e in (0, 1):
            far["f", e] = send(left, left, xp)
        far["s", 1, e] = send(left, left, sib)
        far["m", e].wait_recv()
        if e in (2, 3):
            far["f", e] = send(right, right, xm)
        far["s", 2, e] = send(right, right, sib)

    def across(Y, e, far):
        ref = Y.at[xi[2] * NK + k, yi[e]]
        far["f", e].wait_recv()
        far["s", 3, e] = send(ref, ref, sib)

    def gathered(far):
        for i in range(4):
            for e in range(NY):
                far["s", i, e].wait_recv()

    for n in (3, 4):
        loads[n].wait()
    gcol[...] = column(g_row[...])
    x32 = tok[...].astype(f32)
    ssq[c] = jnp.broadcast_to(jnp.sum(x32 * x32, 0, keepdims=True), (8, TOK))
    for i in range(NY):
        here = slice(i * FR, (i + 1) * FR)
        xsrc[i] = (tok[here].astype(f32) * gcol[here]).astype(bf16)
    for n in (0, 1, 2):
        loads[n].wait()
    pl.semaphore_wait(barrier, len(peers))

    a2x = exchange(xsrc, X)
    ring_p = ring_start(Wp)
    fx, fc = {}, {}
    spread(X, 0, fx)
    sq_sent = [send(ssq.at[c], ssq.at[c], dev) for dev in cols]

    for n in (5, 6, 7, 8, 9):
        loads[n].wait()
    own_docs = jnp.concatenate([docs[pl.ds(2 * row, 1), :], docs[pl.ds(2 * row + 1, 1), :]], 1).astype(f32)
    all_docs = docs[...].astype(f32)
    sign = jnp.ones((1, TOK), f32)
    start = jnp.zeros((1, TOK), f32)
    for d in range(NDOC):
        member = (own_docs == d).astype(f32)
        sign = sign - 2.0 * member * labels[d].astype(f32)
        start = start + member * jnp.sum(
            jnp.sum((all_docs < d).astype(f32), 0, keepdims=True), 1, keepdims=True
        )
    lane = lax.broadcasted_iota(jnp.int32, (1, TOK), 1).astype(f32)
    low = jnp.maximum(start - (row * TOK).astype(f32), lane - (WIN - 1.0))
    for i in range(NY):
        csrc[i] = (ups[i * FR : (i + 1) * FR].astype(f32) * sign).astype(bf16)

    for e in (1, 3):
        a2x[4 - e].wait_recv()
        spread(X, e, fx)
    a2c = exchange(csrc, C)
    onward(X, 0, fx)
    a2x[2].wait_recv()
    spread(X, 2, fx)
    ring_step(Wp, *ring_p, 256)
    half = lax.broadcasted_iota(jnp.int32, (HD // 2, TOK), 0).astype(f32)
    place = lax.broadcasted_iota(jnp.int32, (HD // 2, TOK), 1) + row * TOK
    angles = place.astype(f32) * jnp.exp(half * (-2.0 * math.log(10000.0) / HD))
    cs[0] = jnp.cos(angles)
    cs[1] = jnp.sin(angles)
    onward(X, 1, fx)
    onward(X, 3, fx)
    ring_step(Wp, *ring_p, 256)
    onward(X, 2, fx)
    for e in (1, 3, 2):
        a2c[4 - e].wait_recv()
    for e in (0, 1, 3, 2):
        spread(C, e, fc)
    for e in (0, 1, 3):
        across(X, e, fx)
    ring_step(Wp, *ring_p, 256)
    ring_o = ring_start(Wo)
    across(X, 2, fx)
    gathered(fx)
    onward(C, 0, fc)
    ring_step(Wp, *ring_p, 256)

    def partial(u, e):
        total = None
        for i in range(NC):
            if u < 2:
                t = dot(Wp[i, :, u * 256 : u * 256 + 256], X[i, yi[e]], 0, 0)
            else:
                t = dot(Wo[i], C[i, yi[e]], 0, 0)
            total = t if total is None else total + t
        return total

    def reduce_far(u):
        pq[u, 0] = partial(u, 2).astype(bf16)
        return (
            send(pq.at[u, 0, pl.ds(0, 128)], prh.at[u, 0], yp),
            send(pq.at[u, 0, pl.ds(128, 128)], prh.at[u, 1], ym),
        )

    def reduce_near(u, sent):
        t1 = partial(u, 1)
        t3 = partial(u, 3)
        sent[0].wait_recv()
        pq[u, 1, 0:128] = (t1[0:128] + prh[u, 0].astype(f32)).astype(bf16)
        pq[u, 1, 128:256] = t1[128:256].astype(bf16)
        a = send(pq.at[u, 1], pr.at[u, 0], yp)
        sent[1].wait_recv()
        pq[u, 2, 0:128] = t3[0:128].astype(bf16)
        pq[u, 2, 128:256] = (t3[128:256] + prh[u, 1].astype(f32)).astype(bf16)
        b = send(pq.at[u, 2], pr.at[u, 1], ym)
        return a, b

    def reduced(u, own, sent):
        sent[0].wait_recv()
        sent[1].wait_recv()
        return own + pr[u, 0].astype(f32) + pr[u, 1].astype(f32)

    far_k = reduce_far(1)
    far_q = reduce_far(0)
    near_k = reduce_near(1, far_k)
    ring_step(Wo, *ring_o, 128)
    onward(C, 1, fc)
    near_q = reduce_near(0, far_q)
    own_k = partial(1, 0)
    ring_step(Wo, *ring_o, 128)
    onward(C, 3, fc)
    for s in sq_sent:
        s.wait_recv()
    total_sq = ssq[0, 0:1]
    for i in range(1, NC):
        total_sq = total_sq + ssq[i, 0:1]
    scale = lax.rsqrt(total_sq / D + epsilon)
    co, si = cs[0], cs[1]
    qg, kg = column(qg_row[...]), column(kg_row[...])
    kv_proj = reduced(1, own_k, near_k) * scale
    uk, sk = unit(kv_proj[0:128])
    KV[0, 0:128] = rot(uk * kg, co, si).astype(bf16)
    KV[0, 128:256] = kv_proj[128:256].astype(bf16)
    kv_sent = {4: send(KV.at[0], KV.at[4], zp)}
    later = []
    for e in (1, 3, 2):
        i = count[0]
        count[0] += 1
        first = make(KV.at[0], KV.at[e], {"y": yi[e]}, i)
        second = make(KV.at[4], KV.at[e], {"y": yi[e]}, i)
        pl.when(y + e < NY)(first.start)
        later.append((e, second))
        kv_sent[e] = first
        started.append(first)
    onward(C, 2, fc)
    ring_step(Wo, *ring_o, 128)
    across(C, 0, fc)
    own_q = partial(0, 0)
    q_proj = reduced(0, own_q, near_q) * scale
    kv_sent[4].wait_recv()
    for e, second in later:
        pl.when(y + e >= NY)(second.start)
    across(C, 1, fc)
    across(C, 3, fc)
    ring_step(Wo, *ring_o, 128)
    uq0, sq0 = unit(q_proj[0:128])
    uq1, sq1 = unit(q_proj[128:256])
    q = jnp.concatenate([rot(uq0 * qg, co, si), rot(uq1 * qg, co, si)], 1) * query_scale
    q = q.astype(bf16)
    across(C, 2, fc)
    gathered(fc)
    far_o = reduce_far(2)

    low2 = jnp.concatenate([low, low], 1)
    at2 = jnp.concatenate([lane, lane], 1)
    below = lax.broadcasted_iota(jnp.int32, (TOK, 2 * TOK), 0).astype(f32)

    def scores(d, total, attn):
        s = dot(KV[d, 0:128], q, 0, 0)
        ok = below >= low2 + d * TOK
        if d == 0:
            ok = ok & (below <= at2)
        e = jnp.where(ok, jnp.exp(s), 0.0)
        ex[d] = e
        total = total + jnp.sum(e, 0, keepdims=True)
        return total, attn + dot(KV[d, 128:256], e.astype(bf16), 1, 0)

    total, attn = scores(0, jnp.zeros((1, 2 * TOK), f32), jnp.zeros((HD, 2 * TOK), f32))
    near_o = reduce_near(2, far_o)
    own_o = partial(2, 0)
    for d in (4, 1, 3, 2):
        if d < 4:
            kv_sent[d].wait_recv()
        total, attn = scores(d, total, attn)
    inv = 1.0 / total
    attn = attn * inv
    A[y, 0:128] = attn[:, 0:TOK].astype(bf16)
    A[y, 128:256] = attn[:, TOK:].astype(bf16)

    def ag_start(B):
        return [send(B.at[y], B.at[y], yp), send(B.at[y], B.at[y], ym)]

    def ag_step(B, s):
        s[0].wait_recv()
        low_half = B.at[yi[3], pl.ds(0, 128)]
        s.append(send(low_half, low_half, yp))
        s[1].wait_recv()
        high_half = B.at[yi[1], pl.ds(128, 128)]
        s.append(send(high_half, high_half, ym))

    def ag_end(s):
        s[2].wait_recv()
        s[3].wait_recv()

    da = reduced(2, own_o, near_o)
    ag_a = ag_start(A)
    da = jnp.concatenate([da[0:128], da[128:256]], 1).astype(bf16)
    delta = jnp.sum(attn * da.astype(f32), 0, keepdims=True)
    dq = jnp.zeros((HD, 2 * TOK), f32)
    dkv_sent = {}
    for d in (2, 1, 3, 4, 0):
        p = ex[d] * inv
        dp = dot(KV[d, 128:256], da, 0, 0)
        ds = (p * (dp - delta)).astype(bf16)
        dq = dq + dot(KV[d, 0:128], ds, 1, 0)
        dk = dot(q, ds, 1, 1)
        dv = dot(da, p.astype(bf16), 1, 1)
        if d in (1, 2, 3):
            dsb[d - 1, 0:128] = dk.astype(bf16)
            dsb[d - 1, 128:256] = dv.astype(bf16)
            dkv_sent[d] = send(dsb.at[d - 1], drb.at[d - 1], {"y": yi[NY - d]})
        if d == 4:
            dk4, dv4 = dk, dv
    g0 = unit_back(rot(dq[:, 0:TOK], co, -si) * query_scale * qg, uq0, sq0) * scale
    g1 = unit_back(rot(dq[:, TOK:], co, -si) * query_scale * qg, uq1, sq1) * scale
    Gq[y, 0:128] = g0.astype(bf16)
    Gq[y, 128:256] = g1.astype(bf16)
    ag_step(A, ag_a)
    for d in (1, 3, 2):
        dkv_sent[d].wait_recv()
    for d in (1, 2, 3):
        mine = jnp.where(y + d < NY, 1.0, 0.0)
        gk, gv = drb[d - 1, 0:128].astype(f32), drb[d - 1, 128:256].astype(f32)
        dk, dv = dk + gk * mine, dv + gv * mine
        dk4, dv4 = dk4 + gk * (1.0 - mine), dv4 + gv * (1.0 - mine)
    dsb[3, 0:128] = dk4.astype(bf16)
    dsb[3, 128:256] = dv4.astype(bf16)
    dkv_sent[4] = send(dsb.at[3], drb.at[3], zm)
    ag_q = ag_start(Gq)
    ag_end(ag_a)

    stores = [(C, A), (X, Gq), (X, Gk)]

    def part(u, r):
        L, B = stores[u]
        i = zi[r % NZ]
        left = jnp.concatenate([L[i, j] for j in range(NY)], 1)
        right = jnp.concatenate([B[j] for j in range(NY)], 1)
        return dot(left, right, 1, 1)

    zc = {}

    def zs0(u):
        t = part(u, 4).astype(bf16)
        hb[u, 0] = t[:, 0:128]
        hb[u, 1] = t[:, 128:256]
        zc[u, 0, 0] = send(hb.at[u, 0], hr.at[u, 0], zp)
        zc[u, 1, 0] = send(hb.at[u, 1], hr.at[u, 1], zm)

    def zs1(u):
        t = part(u, 3)
        t3 = part(u, -3)
        zc[u, 0, 0].wait_recv()
        sb[u, 0, 0, :, 0:128] = (t[:, 0:128] + hr[u, 0].astype(f32)).astype(bf16)
        sb[u, 0, 0, :, 128:256] = t[:, 128:256].astype(bf16)
        zc[u, 0, 1] = send(sb.at[u, 0, 0], rb.at[u, 0, 0], zp)
        zc[u, 1, 0].wait_recv()
        sb[u, 1, 0, :, 0:128] = t3[:, 0:128].astype(bf16)
        sb[u, 1, 0, :, 128:256] = (t3[:, 128:256] + hr[u, 1].astype(f32)).astype(bf16)
        zc[u, 1, 1] = send(sb.at[u, 1, 0], rb.at[u, 1, 0], zm)

    def zsn(u, n):
        t = [part(u, 4 - n), part(u, n - 4)]
        for w, dev in enumerate((zp, zm)):
            zc[u, w, n - 1].wait_recv()
            sb[u, w, n - 1] = (t[w] + rb[u, w, n - 2].astype(f32)).astype(bf16)
            zc[u, w, n] = send(sb.at[u, w, n - 1], rb.at[u, w, n - 1], dev)

    def zs4(u):
        t = part(u, 0)
        zc[u, 0, 3].wait_recv()
        zc[u, 1, 3].wait_recv()
        return (t + rb[u, 0, 2].astype(f32) + rb[u, 1, 2].astype(f32)).astype(bf16)

    zs0(0)
    dkv_sent[4].wait_recv()
    dk = dk + drb[3, 0:128].astype(f32)
    dv = dv + drb[3, 128:256].astype(f32)
    gk = unit_back(rot(dk, co, -si) * kg, uk, sk) * scale
    gv = dv * scale
    Gk[y, 0:128] = gk.astype(bf16)
    Gk[y, 128:256] = gv.astype(bf16)
    ag_k = ag_start(Gk)
    inner = jnp.sum(
        g0 * q_proj[0:128] + g1 * q_proj[128:256] + gk * kv_proj[0:128] + gv * kv_proj[128:256], 0, keepdims=True
    )
    inn[c] = jnp.broadcast_to(inner, (8, TOK))
    in_sent = [send(inn.at[c], inn.at[c], dev) for dev in cols]
    ag_step(Gq, ag_q)
    zs1(0)
    ag_end(ag_q)
    zs0(1)
    ag_step(Gk, ag_k)
    zsn(0, 2)
    zs1(1)
    ag_end(ag_k)

    def share(i, j):
        j = yi[j]
        g = jnp.concatenate([Gq[j], Gk[j]], 0)
        return dot(Wp[i], g, 1, 0)

    nc = {}

    def to_sibling(r):
        for j in range(NY):
            nb[r, j] = share(xi[r] * NK + ko, j).astype(bf16)
        nc[r] = send(nb.at[r], nr.at[r], sib)

    to_sibling(2)
    to_sibling(1)
    t2 = [share(xi[2] * NK + k, e) for e in range(NY)]
    nc[2].wait_recv()
    xc = {}
    for e in (1, 2, 0, 3):
        mh[e] = (t2[e] + nr[2, e].astype(f32)).astype(bf16)
        xc[e] = send(mh.at[e], mrh.at[e], xp if e < 2 else xm)
    to_sibling(3)
    zs0(2)
    to_sibling(0)
    zsn(0, 3)
    nc[1].wait_recv()
    nc[3].wait_recv()
    mid = {}

    def middle(w, e):
        r = (1, 3)[w]
        t = share(xi[r] * NK + k, e) + nr[r, e].astype(f32)
        if e // 2 == w:
            xc[e].wait_recv()
            t = t + mrh[e].astype(f32)
        mb[w, e] = t.astype(bf16)
        mid[w, e] = send(mb.at[w, e], mr.at[w, e], (xp, xm)[w])

    middle(0, 2)
    middle(1, 1)
    middle(0, 1)
    middle(1, 2)
    zsn(1, 2)
    zs1(2)
    middle(0, 3)
    middle(1, 0)
    middle(0, 0)
    middle(1, 3)
    g_wo[...] = zs4(0)
    zsn(1, 3)
    zsn(2, 2)
    nc[0].wait_recv()
    back = []
    for e in (2, 1, 3, 0):
        t = share(xi[0] * NK + k, e) + nr[0, e].astype(f32)
        mid[0, e].wait_recv()
        mid[1, e].wait_recv()
        t = (t + mr[0, e].astype(f32) + mr[1, e].astype(f32)).astype(bf16)
        if e:
            ds_[e] = t
            back.append(send(ds_.at[e], dr_.at[y], {"y": yi[e]}))
        else:
            dr_[y] = t
        if e == 2:
            zsn(2, 3)
    g_wq[...] = zs4(1)
    for s in in_sent:
        s.wait_recv()
    in_total = inn[0, 0:1]
    for i in range(1, NC):
        in_total = in_total + inn[i, 0:1]
    factor = scale * in_total / D
    last = zs4(2)
    g_wk[...] = last[:, 0:128]
    g_wv[...] = last[:, 128:256]
    for s in back:
        s.wait_recv()
    for j in range(NY):
        here = slice(j * FR, (j + 1) * FR)
        g_in[here] = (dr_[j].astype(f32) * gcol[here] - tok[here].astype(f32) * factor).astype(bf16)
    for s in started:
        s.wait_send()


def hand_over(*refs):
    n = len(refs) // 2
    for i in range(n):
        refs[n + i][...] = refs[i][...]


def per_device(tokens, input_gain, q_gain, k_gain, wq, wk, wv, wo, upstream, doc_ids, doc_labels):
    V = pltpu.VMEM
    piece = (FR, TOK)
    scratch = [
        V((NY * FR, TOK), bf16), V((NY * FR, TOK), bf16), V((1, NY * FR), f32), V((1, HD), f32), V((1, HD), f32),
        V((NZ * NY * TOK // 128, 128), jnp.int32),
        V((NY,) + piece, bf16), V((NY,) + piece, bf16),
        V((NC, NY) + piece, bf16), V((NC, NY) + piece, bf16),
        V((NZ, FR, 512), bf16), V((NZ, FR, 256), bf16),
        V((NC, 8, TOK), f32), V((NC, 8, TOK), f32), V((NY * FR, 1), f32), V((2, HD // 2, TOK), f32),
        V((3, 3, 256, TOK), bf16), V((3, 2, 256, TOK), bf16), V((3, 2, 128, TOK), bf16),
        V((5, 256, TOK), bf16), V((5, TOK, 2 * TOK), f32),
        V((4, 256, TOK), bf16), V((4, 256, TOK), bf16),
        V((NY, 256, TOK), bf16), V((NY, 256, TOK), bf16), V((NY, 256, TOK), bf16),
        V((3, 2, FR, 128), bf16), V((3, 2, FR, 128), bf16),
        V((3, 2, 3, FR, 256), bf16), V((3, 2, 3, FR, 256), bf16),
        V((NX, NY) + piece, bf16), V((NX, NY) + piece, bf16),
        V((NY,) + piece, bf16), V((NY,) + piece, bf16),
        V((2, NY) + piece, bf16), V((2, NY) + piece, bf16),
        V((NY,) + piece, bf16), V((NY,) + piece, bf16),
        pltpu.SemaphoreType.DMA((10,)), pltpu.SemaphoreType.DMA((NSEM,)), pltpu.SemaphoreType.DMA((NSEM,)),
    ]
    vm = pl.BlockSpec(memory_space=pltpu.VMEM)
    hbm = pl.BlockSpec(memory_space=pl.ANY)
    out = [
        jax.ShapeDtypeStruct((NY * FR, TOK), bf16),
        jax.ShapeDtypeStruct((FR, 256), bf16),
        jax.ShapeDtypeStruct((FR, 128), bf16),
        jax.ShapeDtypeStruct((FR, 128), bf16),
        jax.ShapeDtypeStruct((FR, 256), bf16),
    ]
    results = pl.pallas_call(
        kernel,
        out_shape=out,
        in_specs=[hbm] * 10 + [pl.BlockSpec(memory_space=pltpu.SMEM)],
        out_specs=[vm] * 5,
        scratch_shapes=scratch,
        compiler_params=pltpu.CompilerParams(
            collective_id=0, has_side_effects=True, vmem_limit_bytes=60 * 1024 * 1024
        ),
    )(
        tokens.T, upstream.T, input_gain[None, :], q_gain[None, :], k_gain[None, :], wq, wk, wv, wo,
        doc_ids.reshape(-1, 128), doc_labels,
    )
    results = pl.pallas_call(
        hand_over,
        out_shape=out,
        in_specs=[vm] * 5,
        out_specs=[vm] * 5,
    )(*results)
    return (results[0].T, *results[1:])


def solution(mesh):
    fine = Mesh(mesh.devices.reshape(NZ, NY, NX, NK), ("z", "y", "x", "k"))
    rc = P(("z", "y"), ("x", "k"))
    return jax.shard_map(
        per_device,
        mesh=fine,
        in_specs=(rc, P(("x", "k")), P(), P(), rc, rc, rc, rc, rc, P(), P()),
        out_specs=(rc,) * 5,
        check_vma=False,
    )
```

```python
import math

import jax
import jax.numpy as jnp
from jax import lax
from jax.experimental import pallas as pl
from jax.experimental.pallas import tpu as pltpu
from jax.sharding import Mesh
from jax.sharding import PartitionSpec as P

D = 5376
HD = 128
WIN = 1024
NZ, NY, NX, NK = 8, 4, 4, 2
NC = NX * NK
TOK = 256
FR = 168
NDOC = 8
NSEM = 256
epsilon = 1e-06
query_scale = 168.0 ** (-0.5)
f32 = jnp.float32
bf16 = jnp.bfloat16
MESH = pl.DeviceIdType.MESH


def dot(a, b, ca, cb):
    return lax.dot_general(a, b, (((ca,), (cb,)), ((), ())), preferred_element_type=f32)


def rot(v, c, s):
    a, b = v[: HD // 2], v[HD // 2 :]
    return jnp.concatenate([a * c - b * s, b * c + a * s], 0)


def unit(p):
    sc = lax.rsqrt(jnp.mean(p * p, 0, keepdims=True) + epsilon)
    return p * sc, sc


def unit_back(w, u, sc):
    return sc * (w - u * jnp.mean(w * u, 0, keepdims=True))


def column(v):
    n = v.shape[1]
    parts = []
    for i in range(0, n, 128):
        w = min(128, n - i)
        same = lax.broadcasted_iota(jnp.int32, (w, w), 0) == lax.broadcasted_iota(jnp.int32, (w, w), 1)
        parts.append(jnp.sum(jnp.where(same, v[:, i : i + w], 0.0), 1, keepdims=True))
    return jnp.concatenate(parts, 0) if len(parts) > 1 else parts[0]


def kernel(
    tokens, upstream, gain, q_gain, k_gain, wq, wk, wv, wo, docs_in, labels,
    g_in, g_wq, g_wk, g_wv, g_wo,
    tok, ups, g_row, qg_row, kg_row, docs,
    xsrc, csrc, X, C, Wp, Wo, ssq, inn, gcol, cs,
    pq, pr, prh,
    KV, ex, dsb, drb, A, Gq, Gk,
    hb, hr, sb, rb,
    nb, nr, mh, mrh, mb, mr, ds_, dr_,
    sem_l, sem_s, sem_r,
):
    z, y, x, k = (lax.axis_index(n) for n in ("z", "y", "x", "k"))
    c = x * NK + k
    row = z * NY + y
    zi = [lax.rem(z + r, NZ) for r in range(NZ)]
    yi = [lax.rem(y + r, NY) for r in range(NY)]
    xi = [lax.rem(x + r, NX) for r in range(NX)]
    ko = 1 - k
    zp, zm = {"z": zi[1]}, {"z": zi[NZ - 1]}
    yp, ym = {"y": yi[1]}, {"y": yi[NY - 1]}
    xp, xm = {"x": xi[1]}, {"x": xi[NX - 1]}
    sib = {"k": ko}
    cols = []
    for d in range(1, NC):
        cc = lax.rem(c + d, NC)
        cols.append({"x": cc // NK, "k": lax.rem(cc, NK)})

    barrier = pltpu.get_barrier_semaphore()
    peers = [zp, zm, yp, ym, {"y": yi[2]}] + cols
    for dev in peers:
        pl.semaphore_signal(barrier, inc=1, device_id=dev, device_id_type=MESH)

    loads = []
    for n, (src, dst) in enumerate((
        (wq, Wp.at[z, :, pl.ds(0, 256)]), (wk, Wp.at[z, :, pl.ds(256, 128)]), (wv, Wp.at[z, :, pl.ds(384, 128)]),
        (tokens, tok), (gain, g_row), (docs_in, docs), (upstream, ups), (wo, Wo.at[z]), (q_gain, qg_row), (k_gain, kg_row),
    )):
        loads.append(pltpu.make_async_copy(src, dst, sem_l.at[n]))
        loads[-1].start()

    count = [0]
    started = []

    def make(src, dst, dev, i):
        return pltpu.make_async_remote_copy(
            src_ref=src, dst_ref=dst, send_sem=sem_s.at[i], recv_sem=sem_r.at[i],
            device_id=dev, device_id_type=MESH,
        )

    def send(src, dst, dev):
        i = count[0]
        count[0] += 1
        copy = make(src, dst, dev, i)
        copy.start()
        started.append(copy)
        return copy

    def settle(n):
        for s in started[:n]:
            s.wait_send()
        del started[:n]

    def ring_start(W):
        return [send(W.at[z], W.at[z], zp)], [send(W.at[z], W.at[z], zm)]

    def ring_step(W, fwd, bwd, half):
        s = len(fwd)
        zf, zb = zi[NZ - s], zi[s]
        fwd[-1].wait_recv()
        if s < 3:
            fwd.append(send(W.at[zf], W.at[zf], zp))
        elif s == 3:
            fwd.append(send(W.at[zf, :, pl.ds(0, half)], W.at[zf, :, pl.ds(0, half)], zp))
        bwd[-1].wait_recv()
        if s < 3:
            bwd.append(send(W.at[zb], W.at[zb], zm))
        elif s == 3:
            bwd.append(send(W.at[zb, :, pl.ds(half, half)], W.at[zb, :, pl.ds(half, half)], zm))

    def exchange(src, Y):
        out = {}
        for e in (1, 3, 2):
            out[e] = send(src.at[yi[e]], Y.at[c, y], {"y": yi[e]})
        Y[c, y] = src[yi[0]]
        return out

    def spread(Y, e, far):
        ref = Y.at[c, yi[e]]
        far["p", e] = send(ref, ref, xp)
        far["m", e] = send(ref, ref, xm)
        far["s", 0, e] = send(ref, ref, sib)

    def onward(Y, e, far):
        left = Y.at[xi[NX - 1] * NK + k, yi[e]]
        right = Y.at[xi[1] * NK + k, yi[e]]
        far["p", e].wait_recv()
        if e in (0, 1):
            far["f", e] = send(left, left, xp)
        far["s", 1, e] = send(left, left, sib)
        far["m", e].wait_recv()
        if e in (2, 3):
            far["f", e] = send(right, right, xm)
        far["s", 2, e] = send(right, right, sib)

    def across(Y, e, far):
        ref = Y.at[xi[2] * NK + k, yi[e]]
        far["f", e].wait_recv()
        far["s", 3, e] = send(ref, ref, sib)

    def gathered(far):
        for i in range(4):
            for e in range(NY):
                far["s", i, e].wait_recv()

    for n in (3, 4):
        loads[n].wait()
    gcol[...] = column(g_row[...].reshape(1, NY * FR))
    x32 = tok[...].astype(f32)
    ssq[c] = jnp.broadcast_to(jnp.sum(x32 * x32, 0, keepdims=True), (8, TOK))
    for i in range(NY):
        here = slice(i * FR, (i + 1) * FR)
        xsrc[i] = (tok[here].astype(f32) * gcol[here]).astype(bf16)
    for n in (0, 1, 2):
        loads[n].wait()
    pl.semaphore_wait(barrier, len(peers))

    a2x = exchange(xsrc, X)
    ring_p = ring_start(Wp)
    fx, fc = {}, {}
    spread(X, 0, fx)
    sq_sent = [send(ssq.at[c], ssq.at[c], dev) for dev in cols]

    for n in (5, 6, 7, 8, 9):
        loads[n].wait()
    own_docs = jnp.concatenate([docs[pl.ds(2 * row, 1), :], docs[pl.ds(2 * row + 1, 1), :]], 1).astype(f32)
    all_docs = docs[...].astype(f32)
    sign = jnp.ones((1, TOK), f32)
    start = jnp.zeros((1, TOK), f32)
    for d in range(NDOC):
        member = (own_docs == d).astype(f32)
        sign = sign - 2.0 * member * labels[d].astype(f32)
        start = start + member * jnp.sum(
            jnp.sum((all_docs < d).astype(f32), 0, keepdims=True), 1, keepdims=True
        )
    lane = lax.broadcasted_iota(jnp.int32, (1, TOK), 1).astype(f32)
    low = jnp.maximum(start - (row * TOK).astype(f32), lane - (WIN - 1.0))
    for i in range(NY):
        csrc[i] = (ups[i * FR : (i + 1) * FR].astype(f32) * sign).astype(bf16)

    for e in (1, 3):
        a2x[4 - e].wait_recv()
        spread(X, e, fx)
    a2c = exchange(csrc, C)
    onward(X, 0, fx)
    a2x[2].wait_recv()
    spread(X, 2, fx)
    ring_step(Wp, *ring_p, 256)
    onward(X, 1, fx)
    onward(X, 3, fx)
    ring_step(Wp, *ring_p, 256)
    onward(X, 2, fx)
    for e in (1, 3, 2):
        a2c[4 - e].wait_recv()
    for e in (0, 1, 3, 2):
        spread(C, e, fc)
    for e in (0, 1, 3):
        across(X, e, fx)
    ring_step(Wp, *ring_p, 256)
    ring_o = ring_start(Wo)
    across(X, 2, fx)
    gathered(fx)
    onward(C, 0, fc)
    ring_step(Wp, *ring_p, 256)

    def partial(u, e):
        total = None
        for i in range(NC):
            if u < 2:
                t = dot(Wp[i, :, u * 256 : u * 256 + 256], X[i, yi[e]], 0, 0)
            else:
                t = dot(Wo[i], C[i, yi[e]], 0, 0)
            total = t if total is None else total + t
        return total

    def reduce_far(u):
        pq[u, 0] = partial(u, 2).astype(bf16)
        return (
            send(pq.at[u, 0, pl.ds(0, 128)], prh.at[u, 0], yp),
            send(pq.at[u, 0, pl.ds(128, 128)], prh.at[u, 1], ym),
        )

    def reduce_near(u, sent):
        t1 = partial(u, 1)
        t3 = partial(u, 3)
        sent[0].wait_recv()
        pq[u, 1, 0:128] = (t1[0:128] + prh[u, 0].astype(f32)).astype(bf16)
        pq[u, 1, 128:256] = t1[128:256].astype(bf16)
        a = send(pq.at[u, 1], pr.at[u, 0], yp)
        sent[1].wait_recv()
        pq[u, 2, 0:128] = t3[0:128].astype(bf16)
        pq[u, 2, 128:256] = (t3[128:256] + prh[u, 1].astype(f32)).astype(bf16)
        b = send(pq.at[u, 2], pr.at[u, 1], ym)
        return a, b

    def reduced(u, own, sent):
        sent[0].wait_recv()
        sent[1].wait_recv()
        return own + pr[u, 0].astype(f32) + pr[u, 1].astype(f32)

    old = len(started)
    far_k = reduce_far(1)
    far_q = reduce_far(0)
    half = lax.broadcasted_iota(jnp.int32, (HD // 2, TOK), 0).astype(f32)
    place = lax.broadcasted_iota(jnp.int32, (HD // 2, TOK), 1) + row * TOK
    angles = place.astype(f32) * jnp.exp(half * (-2.0 * math.log(10000.0) / HD))
    cs[0] = jnp.cos(angles)
    cs[1] = jnp.sin(angles)
    near_k = reduce_near(1, far_k)
    ring_step(Wo, *ring_o, 128)
    onward(C, 1, fc)
    own_k = partial(1, 0)
    ring_step(Wo, *ring_o, 128)
    onward(C, 3, fc)
    for s in sq_sent:
        s.wait_recv()
    total_sq = ssq[0, 0:1]
    for i in range(1, NC):
        total_sq = total_sq + ssq[i, 0:1]
    scale = lax.rsqrt(total_sq / D + epsilon)
    co, si = cs[0], cs[1]
    qg, kg = column(qg_row[...]), column(kg_row[...])
    kv_proj = reduced(1, own_k, near_k) * scale
    uk, sk = unit(kv_proj[0:128])
    KV[0, 0:128] = rot(uk * kg, co, si).astype(bf16)
    KV[0, 128:256] = kv_proj[128:256].astype(bf16)
    kv_sent, later = {}, []
    halves = (pl.ds(0, 128), pl.ds(128, 128))
    for h in (0, 1):
        kv_sent[4, h] = send(KV.at[0, halves[h]], KV.at[4, halves[h]], zp)
    for h in (0, 1):
        for e in (1, 3, 2):
            i = count[0]
            count[0] += 1
            first = make(KV.at[0, halves[h]], KV.at[e, halves[h]], {"y": yi[e]}, i)
            second = make(KV.at[4, halves[h]], KV.at[e, halves[h]], {"y": yi[e]}, i)
            pl.when(y + e < NY)(first.start)
            later.append((e, h, second))
            kv_sent[e, h] = first
            started.append(first)
    near_q = reduce_near(0, far_q)
    settle(old)
    onward(C, 2, fc)
    ring_step(Wo, *ring_o, 128)
    across(C, 0, fc)
    own_q = partial(0, 0)
    for h in (0, 1):
        kv_sent[4, h].wait_recv()
        for e, g, second in later:
            if g == h:
                pl.when(y + e >= NY)(second.start)
    q_proj = reduced(0, own_q, near_q) * scale
    across(C, 1, fc)
    across(C, 3, fc)
    ring_step(Wo, *ring_o, 128)
    uq0, sq0 = unit(q_proj[0:128])
    uq1, sq1 = unit(q_proj[128:256])
    q = jnp.concatenate([rot(uq0 * qg, co, si), rot(uq1 * qg, co, si)], 1) * query_scale
    q = q.astype(bf16)
    across(C, 2, fc)
    gathered(fc)
    far_o = reduce_far(2)

    old = len(started)
    low2 = jnp.concatenate([low, low], 1)
    at2 = jnp.concatenate([lane, lane], 1)
    below = lax.broadcasted_iota(jnp.int32, (TOK, 2 * TOK), 0).astype(f32)

    def scores(d, total, attn):
        s = dot(KV[d, 0:128], q, 0, 0)
        ok = below >= low2 + d * TOK
        if d == 0:
            ok = ok & (below <= at2)
        e = jnp.where(ok, jnp.exp(s), 0.0)
        ex[d] = e
        total = total + jnp.sum(e, 0, keepdims=True)
        return total, attn + dot(KV[d, 128:256], e.astype(bf16), 1, 0)

    total, attn = scores(0, jnp.zeros((1, 2 * TOK), f32), jnp.zeros((HD, 2 * TOK), f32))
    near_o = reduce_near(2, far_o)
    own_o = partial(2, 0)
    for d in (4, 1, 3, 2):
        if d < 4:
            kv_sent[d, 0].wait_recv()
            kv_sent[d, 1].wait_recv()
        total, attn = scores(d, total, attn)
    inv = 1.0 / total
    attn = attn * inv
    A[y, 0:128] = attn[:, 0:TOK].astype(bf16)
    A[y, 128:256] = attn[:, TOK:].astype(bf16)

    def ag_start(B):
        return [send(B.at[y], B.at[y], yp), send(B.at[y], B.at[y], ym)]

    def ag_step(B, s):
        s[0].wait_recv()
        low_half = B.at[yi[3], pl.ds(0, 128)]
        s.append(send(low_half, low_half, yp))
        s[1].wait_recv()
        high_half = B.at[yi[1], pl.ds(128, 128)]
        s.append(send(high_half, high_half, ym))

    def ag_end(s):
        s[2].wait_recv()
        s[3].wait_recv()

    da = reduced(2, own_o, near_o)
    ag_a = ag_start(A)
    da = jnp.concatenate([da[0:128], da[128:256]], 1).astype(bf16)
    delta = jnp.sum(attn * da.astype(f32), 0, keepdims=True)
    dq = jnp.zeros((HD, 2 * TOK), f32)
    dkv_sent = {}
    for d in (2, 1, 3, 4, 0):
        p = ex[d] * inv
        dp = dot(KV[d, 128:256], da, 0, 0)
        ds = (p * (dp - delta)).astype(bf16)
        dq = dq + dot(KV[d, 0:128], ds, 1, 0)
        dk = dot(q, ds, 1, 1)
        dv = dot(da, p.astype(bf16), 1, 1)
        if d in (1, 2, 3):
            dsb[d - 1, 0:128] = dk.astype(bf16)
            dsb[d - 1, 128:256] = dv.astype(bf16)
            dkv_sent[d, 0] = send(dsb.at[d - 1, halves[0]], drb.at[d - 1, halves[0]], {"y": yi[NY - d]})
        if d == 4:
            dk4, dv4 = dk, dv
    for d in (2, 1, 3):
        dkv_sent[d, 1] = send(dsb.at[d - 1, halves[1]], drb.at[d - 1, halves[1]], {"y": yi[NY - d]})
    g0 = unit_back(rot(dq[:, 0:TOK], co, -si) * query_scale * qg, uq0, sq0) * scale
    g1 = unit_back(rot(dq[:, TOK:], co, -si) * query_scale * qg, uq1, sq1) * scale
    Gq[y, 0:128] = g0.astype(bf16)
    Gq[y, 128:256] = g1.astype(bf16)
    ag_step(A, ag_a)
    settle(old)
    old = len(started)
    sums = [[dk, dk4], [dv, dv4]]
    for h in (0, 1):
        for d in (1, 3, 2):
            dkv_sent[d, h].wait_recv()
        for d in (1, 2, 3):
            mine = jnp.where(y + d < NY, 1.0, 0.0)
            got = drb[d - 1, h * 128 : h * 128 + 128].astype(f32)
            sums[h][0] = sums[h][0] + got * mine
            sums[h][1] = sums[h][1] + got * (1.0 - mine)
        dsb[3, h * 128 : h * 128 + 128] = sums[h][1].astype(bf16)
        dkv_sent[4, h] = send(dsb.at[3, halves[h]], drb.at[3, halves[h]], zm)
    ag_q = ag_start(Gq)
    ag_end(ag_a)

    stores = [(C, A), (X, Gq), (X, Gk)]

    def part(u, r):
        L, B = stores[u]
        i = zi[r % NZ]
        left = jnp.concatenate([L[i, j] for j in range(NY)], 1)
        right = jnp.concatenate([B[j] for j in range(NY)], 1)
        return dot(left, right, 1, 1)

    zc = {}

    def zs0(u):
        t = part(u, 4).astype(bf16)
        hb[u, 0] = t[:, 0:128]
        hb[u, 1] = t[:, 128:256]
        zc[u, 0, 0] = send(hb.at[u, 0], hr.at[u, 0], zp)
        zc[u, 1, 0] = send(hb.at[u, 1], hr.at[u, 1], zm)

    def zs1(u):
        t = part(u, 3)
        t3 = part(u, -3)
        zc[u, 0, 0].wait_recv()
        sb[u, 0, 0, :, 0:128] = (t[:, 0:128] + hr[u, 0].astype(f32)).astype(bf16)
        sb[u, 0, 0, :, 128:256] = t[:, 128:256].astype(bf16)
        zc[u, 0, 1] = send(sb.at[u, 0, 0], rb.at[u, 0, 0], zp)
        zc[u, 1, 0].wait_recv()
        sb[u, 1, 0, :, 0:128] = t3[:, 0:128].astype(bf16)
        sb[u, 1, 0, :, 128:256] = (t3[:, 128:256] + hr[u, 1].astype(f32)).astype(bf16)
        zc[u, 1, 1] = send(sb.at[u, 1, 0], rb.at[u, 1, 0], zm)

    def zsn(u, n):
        t = [part(u, 4 - n), part(u, n - 4)]
        for w, dev in enumerate((zp, zm)):
            zc[u, w, n - 1].wait_recv()
            sb[u, w, n - 1] = (t[w] + rb[u, w, n - 2].astype(f32)).astype(bf16)
            zc[u, w, n] = send(sb.at[u, w, n - 1], rb.at[u, w, n - 1], dev)

    def zs4(u):
        t = part(u, 0)
        zc[u, 0, 3].wait_recv()
        zc[u, 1, 3].wait_recv()
        return (t + rb[u, 0, 2].astype(f32) + rb[u, 1, 2].astype(f32)).astype(bf16)

    zs0(0)
    def half_start(h):
        ref = Gk.at[y, halves[h]]
        return [send(ref, ref, yp), send(ref, ref, ym)]

    def half_step(h, s):
        s[0].wait_recv()
        ref = Gk.at[yi[3], pl.ds(h * 128, 64)]
        s.append(send(ref, ref, yp))
        s[1].wait_recv()
        ref = Gk.at[yi[1], pl.ds(h * 128 + 64, 64)]
        s.append(send(ref, ref, ym))

    dkv_sent[4, 0].wait_recv()
    dk = sums[0][0] + drb[3, 0:128].astype(f32)
    gk = unit_back(rot(dk, co, -si) * kg, uk, sk) * scale
    Gk[y, 0:128] = gk.astype(bf16)
    ag_k = half_start(0)
    dkv_sent[4, 1].wait_recv()
    gv = (sums[1][0] + drb[3, 128:256].astype(f32)) * scale
    Gk[y, 128:256] = gv.astype(bf16)
    ag_v = half_start(1)
    inner = jnp.sum(
        g0 * q_proj[0:128] + g1 * q_proj[128:256] + gk * kv_proj[0:128] + gv * kv_proj[128:256], 0, keepdims=True
    )
    inn[c] = jnp.broadcast_to(inner, (8, TOK))
    in_sent = [send(inn.at[c], inn.at[c], dev) for dev in cols]
    ag_step(Gq, ag_q)
    zs1(0)
    ag_end(ag_q)
    zs0(1)
    half_step(0, ag_k)
    half_step(1, ag_v)
    zsn(0, 2)
    zs1(1)
    ag_end(ag_k)
    ag_end(ag_v)

    def share(i, j):
        j = yi[j]
        g = jnp.concatenate([Gq[j], Gk[j]], 0)
        return dot(Wp[i], g, 1, 0)

    nc = {}

    def to_sibling(r):
        for j in range(NY):
            nb[r, j] = share(xi[r] * NK + ko, j).astype(bf16)
        nc[r] = send(nb.at[r], nr.at[r], sib)

    to_sibling(2)
    zs0(2)
    to_sibling(1)
    t2 = [share(xi[2] * NK + k, e) for e in range(NY)]
    nc[2].wait_recv()
    xc = {}
    for e in (1, 2, 0, 3):
        mh[e] = (t2[e] + nr[2, e].astype(f32)).astype(bf16)
        xc[e] = send(mh.at[e], mrh.at[e], xp if e < 2 else xm)
    to_sibling(3)
    to_sibling(0)
    zsn(0, 3)
    nc[1].wait_recv()
    nc[3].wait_recv()
    settle(old)
    old = len(started)
    mid = {}

    def middle(w, e):
        r = (1, 3)[w]
        t = share(xi[r] * NK + k, e) + nr[r, e].astype(f32)
        if e // 2 == w:
            xc[e].wait_recv()
            t = t + mrh[e].astype(f32)
        mb[w, e] = t.astype(bf16)
        mid[w, e] = send(mb.at[w, e], mr.at[w, e], (xp, xm)[w])

    middle(0, 2)
    middle(1, 1)
    middle(0, 1)
    middle(1, 2)
    zsn(1, 2)
    zs1(2)
    middle(0, 3)
    middle(1, 3)
    middle(0, 0)
    middle(1, 0)
    zsn(1, 3)
    g_wo[...] = zs4(0)
    zsn(2, 2)
    nc[0].wait_recv()
    settle(old)
    back = []
    for e in (2, 1, 3, 0):
        t = share(xi[0] * NK + k, e) + nr[0, e].astype(f32)
        mid[0, e].wait_recv()
        mid[1, e].wait_recv()
        t = (t + mr[0, e].astype(f32) + mr[1, e].astype(f32)).astype(bf16)
        if e:
            ds_[e] = t
            back.append(send(ds_.at[e], dr_.at[y], {"y": yi[e]}))
        else:
            dr_[y] = t
        if e == 2:
            zsn(2, 3)
    g_wq[...] = zs4(1)
    for s in in_sent:
        s.wait_recv()
    in_total = inn[0, 0:1]
    for i in range(1, NC):
        in_total = in_total + inn[i, 0:1]
    factor = scale * in_total / D
    last = zs4(2)
    g_wk[...] = last[:, 0:128]
    g_wv[...] = last[:, 128:256]
    for s in back:
        s.wait_recv()
    for j in range(NY):
        here = slice(j * FR, (j + 1) * FR)
        g_in[here] = (dr_[j].astype(f32) * gcol[here] - tok[here].astype(f32) * factor).astype(bf16)
    for s in started:
        s.wait_send()


def hand_over(*refs):
    n = len(refs) // 2
    for i in range(n):
        refs[n + i][...] = refs[i][...]


def per_device(tokens, input_gain, q_gain, k_gain, wq, wk, wv, wo, upstream, doc_ids, doc_labels):
    V = pltpu.VMEM
    piece = (FR, TOK)
    scratch = [
        V((NY * FR, TOK), bf16), V((NY * FR, TOK), bf16), V((NY * FR,), f32), V((1, HD), f32), V((1, HD), f32),
        V((NZ * NY * TOK // 128, 128), jnp.int32),
        V((NY,) + piece, bf16), V((NY,) + piece, bf16),
        V((NC, NY) + piece, bf16), V((NC, NY) + piece, bf16),
        V((NZ, FR, 512), bf16), V((NZ, FR, 256), bf16),
        V((NC, 8, TOK), f32), V((NC, 8, TOK), f32), V((NY * FR, 1), f32), V((2, HD // 2, TOK), f32),
        V((3, 3, 256, TOK), bf16), V((3, 2, 256, TOK), bf16), V((3, 2, 128, TOK), bf16),
        V((5, 256, TOK), bf16), V((5, TOK, 2 * TOK), f32),
        V((4, 256, TOK), bf16), V((4, 256, TOK), bf16),
        V((NY, 256, TOK), bf16), V((NY, 256, TOK), bf16), V((NY, 256, TOK), bf16),
        V((3, 2, FR, 128), bf16), V((3, 2, FR, 128), bf16),
        V((3, 2, 3, FR, 256), bf16), V((3, 2, 3, FR, 256), bf16),
        V((NX, NY) + piece, bf16), V((NX, NY) + piece, bf16),
        V((NY,) + piece, bf16), V((NY,) + piece, bf16),
        V((2, NY) + piece, bf16), V((2, NY) + piece, bf16),
        V((NY,) + piece, bf16), V((NY,) + piece, bf16),
        pltpu.SemaphoreType.DMA((10,)), pltpu.SemaphoreType.DMA((NSEM,)), pltpu.SemaphoreType.DMA((NSEM,)),
    ]
    vm = pl.BlockSpec(memory_space=pltpu.VMEM)
    hbm = pl.BlockSpec(memory_space=pl.ANY)
    out = [
        jax.ShapeDtypeStruct((NY * FR, TOK), bf16),
        jax.ShapeDtypeStruct((FR, 256), bf16),
        jax.ShapeDtypeStruct((FR, 128), bf16),
        jax.ShapeDtypeStruct((FR, 128), bf16),
        jax.ShapeDtypeStruct((FR, 256), bf16),
    ]
    results = pl.pallas_call(
        kernel,
        out_shape=out,
        in_specs=[hbm] * 10 + [pl.BlockSpec(memory_space=pltpu.SMEM)],
        out_specs=[vm] * 5,
        scratch_shapes=scratch,
        compiler_params=pltpu.CompilerParams(
            collective_id=0, has_side_effects=True, vmem_limit_bytes=60 * 1024 * 1024
        ),
    )(
        tokens.T, upstream.T, input_gain, q_gain[None, :], k_gain[None, :], wq, wk, wv, wo,
        doc_ids.reshape(-1, 128), doc_labels,
    )
    results = pl.pallas_call(
        hand_over,
        out_shape=out,
        in_specs=[vm] * 5,
        out_specs=[vm] * 5,
    )(*results)
    return (results[0].T, *results[1:])


def solution(mesh):
    fine = Mesh(mesh.devices.reshape(NZ, NY, NX, NK), ("z", "y", "x", "k"))
    rc = P(("z", "y"), ("x", "k"))
    return jax.shard_map(
        per_device,
        mesh=fine,
        in_specs=(rc, P(("x", "k")), P(), P(), rc, rc, rc, rc, rc, P(), P()),
        out_specs=(rc,) * 5,
        check_vma=False,
    )
```

```python
import math

import jax
import jax.numpy as jnp
from jax import lax
from jax.experimental import pallas as pl
from jax.experimental.pallas import tpu as pltpu
from jax.sharding import Mesh
from jax.sharding import PartitionSpec as P

D = 5376
HD = 128
WIN = 1024
NZ, NY, NX, NK = 8, 4, 4, 2
NC = NX * NK
TOK = 256
FR = 168
NDOC = 8
NSEM = 256
epsilon = 1e-06
query_scale = 168.0 ** (-0.5)
f32 = jnp.float32
bf16 = jnp.bfloat16
MESH = pl.DeviceIdType.MESH


def dot(a, b, ca, cb):
    return lax.dot_general(a, b, (((ca,), (cb,)), ((), ())), preferred_element_type=f32)


def rot(v, c, s):
    a, b = v[: HD // 2], v[HD // 2 :]
    return jnp.concatenate([a * c - b * s, b * c + a * s], 0)


def unit(p):
    sc = lax.rsqrt(jnp.mean(p * p, 0, keepdims=True) + epsilon)
    return p * sc, sc


def unit_back(w, u, sc):
    return sc * (w - u * jnp.mean(w * u, 0, keepdims=True))


def column(v):
    n = v.shape[1]
    parts = []
    for i in range(0, n, 128):
        w = min(128, n - i)
        same = lax.broadcasted_iota(jnp.int32, (w, w), 0) == lax.broadcasted_iota(jnp.int32, (w, w), 1)
        parts.append(jnp.sum(jnp.where(same, v[:, i : i + w], 0.0), 1, keepdims=True))
    return jnp.concatenate(parts, 0) if len(parts) > 1 else parts[0]


def kernel(
    tokens, upstream, gain, q_gain, k_gain, wq, wk, wv, wo, docs_in, labels,
    g_in, g_wq, g_wk, g_wv, g_wo,
    tok, ups, g_row, qg_row, kg_row, docs,
    xsrc, csrc, X, C, Wp, Wo, ssq, inn, gcol, cs,
    pq, pr, prh,
    KV, ex, dsb, drb, A, Gq, Gk,
    hb, hr, sb, rb,
    nb, nr, mh, mrh, mb, mr, ds_, dr_,
    sem_l, sem_s, sem_r,
):
    z, y, x, k = (lax.axis_index(n) for n in ("z", "y", "x", "k"))
    c = x * NK + k
    row = z * NY + y
    zi = [lax.rem(z + r, NZ) for r in range(NZ)]
    yi = [lax.rem(y + r, NY) for r in range(NY)]
    xi = [lax.rem(x + r, NX) for r in range(NX)]
    ko = 1 - k
    zp, zm = {"z": zi[1]}, {"z": zi[NZ - 1]}
    yp, ym = {"y": yi[1]}, {"y": yi[NY - 1]}
    xp, xm = {"x": xi[1]}, {"x": xi[NX - 1]}
    sib = {"k": ko}
    cols = []
    for d in range(1, NC):
        cc = lax.rem(c + d, NC)
        cols.append({"x": cc // NK, "k": lax.rem(cc, NK)})

    barrier = pltpu.get_barrier_semaphore()
    peers = [zp, zm, yp, ym, {"y": yi[2]}] + cols
    for dev in peers:
        pl.semaphore_signal(barrier, inc=1, device_id=dev, device_id_type=MESH)

    loads = []
    for n, (src, dst) in enumerate((
        (wq, Wp.at[z, :, pl.ds(0, 256)]), (wk, Wp.at[z, :, pl.ds(256, 128)]), (wv, Wp.at[z, :, pl.ds(384, 128)]),
        (tokens, tok), (gain, g_row), (docs_in, docs), (upstream, ups), (wo, Wo.at[z]), (q_gain, qg_row), (k_gain, kg_row),
    )):
        loads.append(pltpu.make_async_copy(src, dst, sem_l.at[n]))
        loads[-1].start()

    count = [0]
    started = []

    def make(src, dst, dev, i):
        return pltpu.make_async_remote_copy(
            src_ref=src, dst_ref=dst, send_sem=sem_s.at[i], recv_sem=sem_r.at[i],
            device_id=dev, device_id_type=MESH,
        )

    def send(src, dst, dev):
        i = count[0]
        count[0] += 1
        copy = make(src, dst, dev, i)
        copy.start()
        started.append(copy)
        return copy

    def settle(n):
        for s in started[:n]:
            s.wait_send()
        del started[:n]

    def ring_start(W):
        return [send(W.at[z], W.at[z], zp)], [send(W.at[z], W.at[z], zm)]

    def ring_step(W, fwd, bwd, half):
        s = len(fwd)
        zf, zb = zi[NZ - s], zi[s]
        fwd[-1].wait_recv()
        if s < 3:
            fwd.append(send(W.at[zf], W.at[zf], zp))
        elif s == 3:
            fwd.append(send(W.at[zf, :, pl.ds(0, half)], W.at[zf, :, pl.ds(0, half)], zp))
        bwd[-1].wait_recv()
        if s < 3:
            bwd.append(send(W.at[zb], W.at[zb], zm))
        elif s == 3:
            bwd.append(send(W.at[zb, :, pl.ds(half, half)], W.at[zb, :, pl.ds(half, half)], zm))

    def exchange(src, Y):
        out = {}
        for e in (1, 3, 2):
            out[e] = send(src.at[yi[e]], Y.at[c, y], {"y": yi[e]})
        Y[c, y] = src[yi[0]]
        return out

    def spread(Y, e, far):
        ref = Y.at[c, yi[e]]
        far["p", e] = send(ref, ref, xp)
        far["m", e] = send(ref, ref, xm)
        far["s", 0, e] = send(ref, ref, sib)

    def onward(Y, e, far):
        left = Y.at[xi[NX - 1] * NK + k, yi[e]]
        right = Y.at[xi[1] * NK + k, yi[e]]
        far["p", e].wait_recv()
        if e in (0, 1):
            far["f", e] = send(left, left, xp)
        far["s", 1, e] = send(left, left, sib)
        far["m", e].wait_recv()
        if e in (2, 3):
            far["f", e] = send(right, right, xm)
        far["s", 2, e] = send(right, right, sib)

    def across(Y, e, far):
        ref = Y.at[xi[2] * NK + k, yi[e]]
        far["f", e].wait_recv()
        far["s", 3, e] = send(ref, ref, sib)

    def gathered(far):
        for i in range(4):
            for e in range(NY):
                far["s", i, e].wait_recv()

    for n in (3, 4):
        loads[n].wait()
    gcol[...] = column(g_row[...].reshape(1, NY * FR))
    x32 = tok[...].astype(f32)
    ssq[c] = jnp.broadcast_to(jnp.sum(x32 * x32, 0, keepdims=True), (8, TOK))
    for i in range(NY):
        here = slice(i * FR, (i + 1) * FR)
        xsrc[i] = (tok[here].astype(f32) * gcol[here]).astype(bf16)
    for n in (0, 1, 2):
        loads[n].wait()
    pl.semaphore_wait(barrier, len(peers))

    a2x = exchange(xsrc, X)
    ring_p = ring_start(Wp)
    fx, fc = {}, {}
    spread(X, 0, fx)
    sq_sent = [send(ssq.at[c], ssq.at[c], dev) for dev in cols]

    for n in (5, 6, 7, 8, 9):
        loads[n].wait()
    own_docs = jnp.concatenate([docs[pl.ds(2 * row, 1), :], docs[pl.ds(2 * row + 1, 1), :]], 1).astype(f32)
    all_docs = docs[...].astype(f32)
    sign = jnp.ones((1, TOK), f32)
    start = jnp.zeros((1, TOK), f32)
    for d in range(NDOC):
        member = (own_docs == d).astype(f32)
        sign = sign - 2.0 * member * labels[d].astype(f32)
        start = start + member * jnp.sum(
            jnp.sum((all_docs < d).astype(f32), 0, keepdims=True), 1, keepdims=True
        )
    lane = lax.broadcasted_iota(jnp.int32, (1, TOK), 1).astype(f32)
    low = jnp.maximum(start - (row * TOK).astype(f32), lane - (WIN - 1.0))
    for i in range(NY):
        csrc[i] = (ups[i * FR : (i + 1) * FR].astype(f32) * sign).astype(bf16)

    for e in (1, 3):
        a2x[4 - e].wait_recv()
        spread(X, e, fx)
    a2c = exchange(csrc, C)
    onward(X, 0, fx)
    a2x[2].wait_recv()
    spread(X, 2, fx)
    ring_step(Wp, *ring_p, 256)
    onward(X, 1, fx)
    onward(X, 3, fx)
    ring_step(Wp, *ring_p, 256)
    onward(X, 2, fx)
    for e in (1, 3, 2):
        a2c[4 - e].wait_recv()
    for e in (0, 1, 3, 2):
        spread(C, e, fc)
    for e in (0, 1, 3):
        across(X, e, fx)
    ring_step(Wp, *ring_p, 256)
    ring_o = ring_start(Wo)
    across(X, 2, fx)
    gathered(fx)
    onward(C, 0, fc)
    ring_step(Wp, *ring_p, 256)

    def partial(u, e):
        total = None
        for i in range(NC):
            if u < 2:
                t = dot(Wp[i, :, u * 256 : u * 256 + 256], X[i, yi[e]], 0, 0)
            else:
                t = dot(Wo[i], C[i, yi[e]], 0, 0)
            total = t if total is None else total + t
        return total

    def reduce_far(u):
        pq[u, 0] = partial(u, 2).astype(bf16)
        return (
            send(pq.at[u, 0, pl.ds(0, 128)], prh.at[u, 0], yp),
            send(pq.at[u, 0, pl.ds(128, 128)], prh.at[u, 1], ym),
        )

    def reduce_near(u, sent):
        t1 = partial(u, 1)
        t3 = partial(u, 3)
        sent[0].wait_recv()
        pq[u, 1, 0:128] = (t1[0:128] + prh[u, 0].astype(f32)).astype(bf16)
        pq[u, 1, 128:256] = t1[128:256].astype(bf16)
        a = send(pq.at[u, 1], pr.at[u, 0], yp)
        sent[1].wait_recv()
        pq[u, 2, 0:128] = t3[0:128].astype(bf16)
        pq[u, 2, 128:256] = (t3[128:256] + prh[u, 1].astype(f32)).astype(bf16)
        b = send(pq.at[u, 2], pr.at[u, 1], ym)
        return a, b

    def reduced(u, own, sent):
        sent[0].wait_recv()
        sent[1].wait_recv()
        return own + pr[u, 0].astype(f32) + pr[u, 1].astype(f32)

    old = len(started)
    far_k = reduce_far(1)
    far_q = reduce_far(0)
    half = lax.broadcasted_iota(jnp.int32, (HD // 2, TOK), 0).astype(f32)
    place = lax.broadcasted_iota(jnp.int32, (HD // 2, TOK), 1) + row * TOK
    angles = place.astype(f32) * jnp.exp(half * (-2.0 * math.log(10000.0) / HD))
    cs[0] = jnp.cos(angles)
    cs[1] = jnp.sin(angles)
    near_k = reduce_near(1, far_k)
    ring_step(Wo, *ring_o, 128)
    onward(C, 1, fc)
    own_k = partial(1, 0)
    ring_step(Wo, *ring_o, 128)
    onward(C, 3, fc)
    for s in sq_sent:
        s.wait_recv()
    total_sq = ssq[0, 0:1]
    for i in range(1, NC):
        total_sq = total_sq + ssq[i, 0:1]
    scale = lax.rsqrt(total_sq / D + epsilon)
    co, si = cs[0], cs[1]
    qg, kg = column(qg_row[...]), column(kg_row[...])
    kv_proj = reduced(1, own_k, near_k) * scale
    uk, sk = unit(kv_proj[0:128])
    KV[0, 0:128] = rot(uk * kg, co, si).astype(bf16)
    KV[0, 128:256] = kv_proj[128:256].astype(bf16)
    kv_sent, later = {}, []
    halves = (pl.ds(0, 128), pl.ds(128, 128))
    for h in (0, 1):
        kv_sent[4, h] = send(KV.at[0, halves[h]], KV.at[4, halves[h]], zp)
    for h in (0, 1):
        for e in (1, 3, 2):
            i = count[0]
            count[0] += 1
            first = make(KV.at[0, halves[h]], KV.at[e, halves[h]], {"y": yi[e]}, i)
            second = make(KV.at[4, halves[h]], KV.at[e, halves[h]], {"y": yi[e]}, i)
            pl.when(y + e < NY)(first.start)
            later.append((e, h, second))
            kv_sent[e, h] = first
            started.append(first)
    near_q = reduce_near(0, far_q)
    settle(old)
    onward(C, 2, fc)
    ring_step(Wo, *ring_o, 128)
    across(C, 0, fc)
    own_q = partial(0, 0)
    for h in (0, 1):
        kv_sent[4, h].wait_recv()
        for e, g, second in later:
            if g == h:
                pl.when(y + e >= NY)(second.start)
    q_proj = reduced(0, own_q, near_q) * scale
    across(C, 1, fc)
    across(C, 3, fc)
    ring_step(Wo, *ring_o, 128)
    uq0, sq0 = unit(q_proj[0:128])
    uq1, sq1 = unit(q_proj[128:256])
    q = jnp.concatenate([rot(uq0 * qg, co, si), rot(uq1 * qg, co, si)], 1) * query_scale
    q = q.astype(bf16)
    across(C, 2, fc)
    gathered(fc)
    far_o = reduce_far(2)

    old = len(started)
    low2 = jnp.concatenate([low, low], 1)
    at2 = jnp.concatenate([lane, lane], 1)
    below = lax.broadcasted_iota(jnp.int32, (TOK, 2 * TOK), 0).astype(f32)

    def scores(d, total, attn):
        s = dot(KV[d, 0:128], q, 0, 0)
        ok = below >= low2 + d * TOK
        if d == 0:
            ok = ok & (below <= at2)
        e = jnp.where(ok, jnp.exp(s), 0.0)
        ex[d] = e
        total = total + jnp.sum(e, 0, keepdims=True)
        return total, attn + dot(KV[d, 128:256], e.astype(bf16), 1, 0)

    total, attn = scores(0, jnp.zeros((1, 2 * TOK), f32), jnp.zeros((HD, 2 * TOK), f32))
    near_o = reduce_near(2, far_o)
    own_o = partial(2, 0)
    for d in (4, 1, 3, 2):
        if d < 4:
            kv_sent[d, 0].wait_recv()
            kv_sent[d, 1].wait_recv()
        total, attn = scores(d, total, attn)
    inv = 1.0 / total
    attn = attn * inv
    A[y, 0:128] = attn[:, 0:TOK].astype(bf16)
    A[y, 128:256] = attn[:, TOK:].astype(bf16)

    def ag_start(B):
        return [send(B.at[y], B.at[y], yp), send(B.at[y], B.at[y], ym)]

    def ag_step(B, s):
        s[0].wait_recv()
        low_half = B.at[yi[3], pl.ds(0, 128)]
        s.append(send(low_half, low_half, yp))
        s[1].wait_recv()
        high_half = B.at[yi[1], pl.ds(128, 128)]
        s.append(send(high_half, high_half, ym))

    def ag_end(s):
        s[2].wait_recv()
        s[3].wait_recv()

    da = reduced(2, own_o, near_o)
    ag_a = ag_start(A)
    da = jnp.concatenate([da[0:128], da[128:256]], 1).astype(bf16)
    delta = jnp.sum(attn * da.astype(f32), 0, keepdims=True)
    dq = jnp.zeros((HD, 2 * TOK), f32)
    dkv_sent = {}
    for d in (2, 1, 3, 4, 0):
        p = ex[d] * inv
        dp = dot(KV[d, 128:256], da, 0, 0)
        ds = (p * (dp - delta)).astype(bf16)
        dq = dq + dot(KV[d, 0:128], ds, 1, 0)
        dk = dot(q, ds, 1, 1)
        dv = dot(da, p.astype(bf16), 1, 1)
        if d in (1, 2, 3):
            dsb[d - 1, 0:128] = dk.astype(bf16)
            dsb[d - 1, 128:256] = dv.astype(bf16)
            dkv_sent[d, 0] = send(dsb.at[d - 1, halves[0]], drb.at[d - 1, halves[0]], {"y": yi[NY - d]})
        if d == 4:
            dk4, dv4 = dk, dv
    for d in (2, 1, 3):
        dkv_sent[d, 1] = send(dsb.at[d - 1, halves[1]], drb.at[d - 1, halves[1]], {"y": yi[NY - d]})
    g0 = unit_back(rot(dq[:, 0:TOK], co, -si) * query_scale * qg, uq0, sq0) * scale
    g1 = unit_back(rot(dq[:, TOK:], co, -si) * query_scale * qg, uq1, sq1) * scale
    Gq[y, 0:128] = g0.astype(bf16)
    Gq[y, 128:256] = g1.astype(bf16)
    ag_step(A, ag_a)
    settle(old)
    old = len(started)
    sums = [[dk, dk4], [dv, dv4]]
    for h in (0, 1):
        for d in (1, 3, 2):
            dkv_sent[d, h].wait_recv()
        for d in (1, 2, 3):
            mine = jnp.where(y + d < NY, 1.0, 0.0)
            got = drb[d - 1, h * 128 : h * 128 + 128].astype(f32)
            sums[h][0] = sums[h][0] + got * mine
            sums[h][1] = sums[h][1] + got * (1.0 - mine)
        dsb[3, h * 128 : h * 128 + 128] = sums[h][1].astype(bf16)
        dkv_sent[4, h] = send(dsb.at[3, halves[h]], drb.at[3, halves[h]], zm)
    ag_q = ag_start(Gq)
    ag_end(ag_a)

    stores = [(C, A), (X, Gq), (X, Gk)]

    def part(u, r):
        L, B = stores[u]
        i = zi[r % NZ]
        left = jnp.concatenate([L[i, j] for j in range(NY)], 1)
        right = jnp.concatenate([B[j] for j in range(NY)], 1)
        return dot(left, right, 1, 1)

    zc = {}

    def zs0(u):
        t = part(u, 4).astype(bf16)
        hb[u, 0] = t[:, 0:128]
        hb[u, 1] = t[:, 128:256]
        zc[u, 0, 0] = send(hb.at[u, 0], hr.at[u, 0], zp)
        zc[u, 1, 0] = send(hb.at[u, 1], hr.at[u, 1], zm)

    def zs1(u):
        t = part(u, 3)
        t3 = part(u, -3)
        zc[u, 0, 0].wait_recv()
        sb[u, 0, 0, :, 0:128] = (t[:, 0:128] + hr[u, 0].astype(f32)).astype(bf16)
        sb[u, 0, 0, :, 128:256] = t[:, 128:256].astype(bf16)
        zc[u, 0, 1] = send(sb.at[u, 0, 0], rb.at[u, 0, 0], zp)
        zc[u, 1, 0].wait_recv()
        sb[u, 1, 0, :, 0:128] = t3[:, 0:128].astype(bf16)
        sb[u, 1, 0, :, 128:256] = (t3[:, 128:256] + hr[u, 1].astype(f32)).astype(bf16)
        zc[u, 1, 1] = send(sb.at[u, 1, 0], rb.at[u, 1, 0], zm)

    def zsn(u, n):
        t = [part(u, 4 - n), part(u, n - 4)]
        for w, dev in enumerate((zp, zm)):
            zc[u, w, n - 1].wait_recv()
            sb[u, w, n - 1] = (t[w] + rb[u, w, n - 2].astype(f32)).astype(bf16)
            zc[u, w, n] = send(sb.at[u, w, n - 1], rb.at[u, w, n - 1], dev)

    def zs4(u):
        t = part(u, 0)
        zc[u, 0, 3].wait_recv()
        zc[u, 1, 3].wait_recv()
        return (t + rb[u, 0, 2].astype(f32) + rb[u, 1, 2].astype(f32)).astype(bf16)

    zs0(0)
    def half_start(h):
        ref = Gk.at[y, halves[h]]
        return [send(ref, ref, yp), send(ref, ref, ym)]

    def half_step(h, s):
        s[0].wait_recv()
        ref = Gk.at[yi[3], pl.ds(h * 128, 64)]
        s.append(send(ref, ref, yp))
        s[1].wait_recv()
        ref = Gk.at[yi[1], pl.ds(h * 128 + 64, 64)]
        s.append(send(ref, ref, ym))

    dkv_sent[4, 0].wait_recv()
    dk = sums[0][0] + drb[3, 0:128].astype(f32)
    gk = unit_back(rot(dk, co, -si) * kg, uk, sk) * scale
    Gk[y, 0:128] = gk.astype(bf16)
    ag_k = half_start(0)
    dkv_sent[4, 1].wait_recv()
    gv = (sums[1][0] + drb[3, 128:256].astype(f32)) * scale
    Gk[y, 128:256] = gv.astype(bf16)
    ag_v = half_start(1)
    inner = jnp.sum(
        g0 * q_proj[0:128] + g1 * q_proj[128:256] + gk * kv_proj[0:128] + gv * kv_proj[128:256], 0, keepdims=True
    )
    inn[c] = jnp.broadcast_to(inner, (8, TOK))
    in_sent = [send(inn.at[c], inn.at[c], dev) for dev in cols]
    ag_step(Gq, ag_q)
    zs1(0)
    ag_end(ag_q)
    zs0(1)
    half_step(0, ag_k)
    half_step(1, ag_v)
    zsn(0, 2)
    zs1(1)
    ag_end(ag_k)
    ag_end(ag_v)

    def share(i, j):
        j = yi[j]
        g = jnp.concatenate([Gq[j], Gk[j]], 0)
        return dot(Wp[i], g, 1, 0)

    nc = {}

    def to_sibling(r):
        for j in range(NY):
            nb[r, j] = share(xi[r] * NK + ko, j).astype(bf16)
        nc[r] = send(nb.at[r], nr.at[r], sib)

    to_sibling(2)
    zs0(2)
    t2 = [share(xi[2] * NK + k, e) for e in range(NY)]
    nc[2].wait_recv()
    xc = {}
    for e in (1, 2, 0, 3):
        mh[e] = (t2[e] + nr[2, e].astype(f32)).astype(bf16)
        xc[e] = send(mh.at[e], mrh.at[e], xp if e < 2 else xm)
    to_sibling(1)
    to_sibling(3)
    to_sibling(0)
    zsn(0, 3)
    nc[1].wait_recv()
    nc[3].wait_recv()
    settle(old)
    old = len(started)
    mid = {}

    def middle(w, e):
        r = (1, 3)[w]
        t = share(xi[r] * NK + k, e) + nr[r, e].astype(f32)
        if e // 2 == w:
            xc[e].wait_recv()
            t = t + mrh[e].astype(f32)
        mb[w, e] = t.astype(bf16)
        mid[w, e] = send(mb.at[w, e], mr.at[w, e], (xp, xm)[w])

    middle(0, 2)
    middle(1, 1)
    middle(0, 1)
    middle(1, 2)
    zsn(1, 2)
    zs1(2)
    middle(0, 3)
    middle(1, 3)
    middle(0, 0)
    middle(1, 0)
    zsn(1, 3)
    g_wo[...] = zs4(0)
    zsn(2, 2)
    nc[0].wait_recv()
    settle(old)
    back = []
    for e in (2, 1, 3, 0):
        t = share(xi[0] * NK + k, e) + nr[0, e].astype(f32)
        mid[0, e].wait_recv()
        mid[1, e].wait_recv()
        t = (t + mr[0, e].astype(f32) + mr[1, e].astype(f32)).astype(bf16)
        if e:
            ds_[e] = t
            back.append(send(ds_.at[e], dr_.at[y], {"y": yi[e]}))
        else:
            dr_[y] = t
        if e == 2:
            zsn(2, 3)
    g_wq[...] = zs4(1)
    for s in in_sent:
        s.wait_recv()
    in_total = inn[0, 0:1]
    for i in range(1, NC):
        in_total = in_total + inn[i, 0:1]
    factor = scale * in_total / D
    last = zs4(2)
    g_wk[...] = last[:, 0:128]
    g_wv[...] = last[:, 128:256]
    for s in back:
        s.wait_recv()
    for j in range(NY):
        here = slice(j * FR, (j + 1) * FR)
        g_in[here] = (dr_[j].astype(f32) * gcol[here] - tok[here].astype(f32) * factor).astype(bf16)
    for s in started:
        s.wait_send()


def hand_over(*refs):
    n = len(refs) // 2
    for i in range(n):
        refs[n + i][...] = refs[i][...]


def per_device(tokens, input_gain, q_gain, k_gain, wq, wk, wv, wo, upstream, doc_ids, doc_labels):
    V = pltpu.VMEM
    piece = (FR, TOK)
    scratch = [
        V((NY * FR, TOK), bf16), V((NY * FR, TOK), bf16), V((NY * FR,), f32), V((1, HD), f32), V((1, HD), f32),
        V((NZ * NY * TOK // 128, 128), jnp.int32),
        V((NY,) + piece, bf16), V((NY,) + piece, bf16),
        V((NC, NY) + piece, bf16), V((NC, NY) + piece, bf16),
        V((NZ, FR, 512), bf16), V((NZ, FR, 256), bf16),
        V((NC, 8, TOK), f32), V((NC, 8, TOK), f32), V((NY * FR, 1), f32), V((2, HD // 2, TOK), f32),
        V((3, 3, 256, TOK), bf16), V((3, 2, 256, TOK), bf16), V((3, 2, 128, TOK), bf16),
        V((5, 256, TOK), bf16), V((5, TOK, 2 * TOK), f32),
        V((4, 256, TOK), bf16), V((4, 256, TOK), bf16),
        V((NY, 256, TOK), bf16), V((NY, 256, TOK), bf16), V((NY, 256, TOK), bf16),
        V((3, 2, FR, 128), bf16), V((3, 2, FR, 128), bf16),
        V((3, 2, 3, FR, 256), bf16), V((3, 2, 3, FR, 256), bf16),
        V((NX, NY) + piece, bf16), V((NX, NY) + piece, bf16),
        V((NY,) + piece, bf16), V((NY,) + piece, bf16),
        V((2, NY) + piece, bf16), V((2, NY) + piece, bf16),
        V((NY,) + piece, bf16), V((NY,) + piece, bf16),
        pltpu.SemaphoreType.DMA((10,)), pltpu.SemaphoreType.DMA((NSEM,)), pltpu.SemaphoreType.DMA((NSEM,)),
    ]
    vm = pl.BlockSpec(memory_space=pltpu.VMEM)
    hbm = pl.BlockSpec(memory_space=pl.ANY)
    out = [
        jax.ShapeDtypeStruct((NY * FR, TOK), bf16),
        jax.ShapeDtypeStruct((FR, 256), bf16),
        jax.ShapeDtypeStruct((FR, 128), bf16),
        jax.ShapeDtypeStruct((FR, 128), bf16),
        jax.ShapeDtypeStruct((FR, 256), bf16),
    ]
    results = pl.pallas_call(
        kernel,
        out_shape=out,
        in_specs=[hbm] * 10 + [pl.BlockSpec(memory_space=pltpu.SMEM)],
        out_specs=[vm] * 5,
        scratch_shapes=scratch,
        compiler_params=pltpu.CompilerParams(
            collective_id=0, has_side_effects=True, vmem_limit_bytes=60 * 1024 * 1024
        ),
    )(
        tokens.T, upstream.T, input_gain, q_gain[None, :], k_gain[None, :], wq, wk, wv, wo,
        doc_ids.reshape(-1, 128), doc_labels,
    )
    results = pl.pallas_call(
        hand_over,
        out_shape=out,
        in_specs=[vm] * 5,
        out_specs=[vm] * 5,
    )(*results)
    return (results[0].T, *results[1:])


def solution(mesh):
    fine = Mesh(mesh.devices.reshape(NZ, NY, NX, NK), ("z", "y", "x", "k"))
    rc = P(("z", "y"), ("x", "k"))
    return jax.shard_map(
        per_device,
        mesh=fine,
        in_specs=(rc, P(("x", "k")), P(), P(), rc, rc, rc, rc, rc, P(), P()),
        out_specs=(rc,) * 5,
        check_vma=False,
    )
```
